32 devices in a mesh: row: 4 (over y, x), col: 8 (over z, core).
Axes of the slice: x: 2, y: 2, z: 4, core: 2. Of those that a mesh axis runs over, the one named last changes fastest.
Arguments:
- blocks: bfloat16 [32, 48, 128, 128], P('row', 'col'), as said below
- col_index: int32 [32, 48], P('row', 'col'), may hold values from -1 to 31, as said below
- vectors: float32 [4096, 256], P(('col', 'row')), may hold values from -6 to 6
Outputs:
- orbitals: float32 [4096, 256], P(('col', 'row'))
The draws below stay inside these ranges and needn't reach their ends.
Inputs may be any that keep to these rules, and one draw needn't show every extreme that they name: `col_index`: entry [I, c * 6 + t] is the global index of a nonzero block of block row I that lies in column group c (block columns c * 4 to (c + 1) * 4 - 1), or -1 for an empty slot; within one row and group the listed blocks come first and are distinct. The pattern is symmetric (J is listed in row I exactly when I is listed in row J) and every row lists its diagonal block. At most 4 blocks of one row lie in one column group, and some rows have exactly 4 there. `blocks`: H is symmetric: the block listed for (J, I) is the transpose of the block listed for (I, J). Blocks in empty slots are not part of H.
All inputs are finite; a program needn't handle non-finite values.
Results may differ from the reference program's by a relative error of at most 0.006.
Values may be sent and summed in bfloat16 or wider, within the bound.
No kernel may reach another device: no remote copies, remote signals or barrier semaphores. Data moves between devices by JAX's collectives and lax.ppermute only.
A program may use at most 128 MiB of HBM per device.

```python
import math
import jax
import jax.numpy as jnp
from jax import lax

BLOCK = 128
STATES = 256
SLOTS = 6
DEGREE = 4
NBLK = 32
NORB = 4096
TILE = 4
KMAX = 4
N_COL = 8


def block_pattern(key):
    tiles = N_COL
    key_counts = jax.random.fold_in(key, 101)
    key_heavy = jax.random.fold_in(key, 102)
    key_other = jax.random.fold_in(key, 103)
    key_near = jax.random.fold_in(key, 104)
    key_order = jax.random.fold_in(key, 105)
    key_spread = jax.random.fold_in(key, 106)
    drawn = jax.random.randint(key_counts, (tiles, tiles), 0, KMAX + 1)
    skewed = 2 + drawn * (KMAX - 2) // KMAX
    upper_part = jnp.triu(skewed, 1)
    counts = upper_part + upper_part.T
    heavy_a = jax.random.randint(key_heavy, (), 0, tiles)
    heavy_b = (heavy_a + 1 + jax.random.randint(key_other, (), 0, tiles - 1)) % tiles
    counts = counts.at[heavy_a, heavy_b].set(KMAX)
    counts = counts.at[heavy_b, heavy_a].set(KMAX)
    near_most = min((SLOTS - 1) // 2, (TILE - 1) // 2)
    half_span = max((TILE - 1) // 2, 1)
    near = jax.random.randint(key_near, (tiles,), 0, near_most + 1)
    scores = jax.random.randint(key_order, (tiles, tiles, TILE), 0, 1 << 20) * TILE + jnp.arange(TILE, dtype=jnp.int32)
    order = jnp.argsort(scores, axis=-1).astype(jnp.int32)
    spread_scores = jax.random.randint(key_spread, (tiles, half_span), 0, 1 << 20) * half_span + jnp.arange(half_span, dtype=jnp.int32)
    spread = jnp.argsort(spread_scores, axis=-1).astype(jnp.int32) + 1
    rows = jnp.arange(NBLK, dtype=jnp.int32)
    slot_ids = jnp.arange(N_COL * SLOTS, dtype=jnp.int32)
    tile_row = (rows // TILE)[:, None]
    inner = (rows % TILE)[:, None]
    tile_col = (slot_ids // SLOTS)[None, :]
    within = (slot_ids % SLOTS)[None, :]
    low_tile = jnp.minimum(tile_row, tile_col)
    high_tile = jnp.maximum(tile_row, tile_col)
    offset = order[low_tile, high_tile, jnp.minimum(within, TILE - 1)]
    direction = jnp.where(tile_row < tile_col, 1, -1)
    far_col = (inner + direction * offset) % TILE
    far_live = within < counts[tile_row, tile_col]
    rank_index = jnp.clip((within + 1) // 2 - 1, 0, half_span - 1)
    distance = spread[tile_row, rank_index]
    turning = jnp.where(within % 2 == 1, 1, -1)
    near_col = jnp.where(within == 0, inner, (inner + turning * distance) % TILE)
    near_live = within < 1 + 2 * near[tile_row]
    same_tile = tile_row == tile_col
    local_col = jnp.where(same_tile, near_col, far_col)
    is_live = jnp.where(same_tile, near_live, far_live)
    target = tile_col * TILE + local_col
    col_index = jnp.where(is_live, target, -1).astype(jnp.int32)
    mate = jnp.where(same_tile, jnp.where(within == 0, within, jnp.where(within % 2 == 1, within + 1, within - 1)), within)
    mate_slot = jnp.where(is_live, tile_row * SLOTS + mate, 0)
    mate_row = jnp.where(is_live, target, 0)
    selfish = same_tile & (within == 0) & is_live
    keeping = (tile_row < tile_col) | same_tile & (within % 2 == 1) | jnp.logical_not(is_live)
    return (col_index, mate_row, mate_slot, keeping, selfish)


def draw_col_index(key, part):
    pattern_parts = block_pattern(key)
    return pattern_parts[0]


def draw_blocks(key, part):
    col_index, mate_row, mate_slot, keeping, selfish = block_pattern(key)
    key = jax.random.fold_in(key, 7)
    scale = 1.0 / math.sqrt(BLOCK * (2.0 * N_COL * KMAX / 3.0 + 2.0))
    shape = (NBLK, N_COL * SLOTS, BLOCK, BLOCK)
    raw = jax.random.normal(key, shape, jnp.float32) * scale
    mirrored = jnp.swapaxes(raw[mate_row, mate_slot], -1, -2)
    balanced = (raw + jnp.swapaxes(raw, -1, -2)) * 0.70710678
    values = jnp.where(keeping[:, :, None, None], raw, mirrored)
    values = jnp.where(selfish[:, :, None, None], balanced, values)
    return values.astype(jnp.bfloat16)


def level_of(key, shape, split, low, largest):
    factor_of = 1.0
    for axis_at, parts in split:
        draws = jax.random.uniform(jax.random.fold_in(jax.random.fold_in(key, 6), axis_at), (parts,), jnp.float32, low / len(split), largest / len(split))
        factor_of = factor_of * jnp.repeat(jnp.exp(draws), shape[axis_at] // parts).reshape((-1,) + (1,) * (len(shape) - 1 - axis_at))
    return factor_of


def scatter_about(rng, extent, scale, limit, shards=(), held_as=jnp.bfloat16):
    array = jax.random.normal(rng, extent, jnp.float32) * scale
    if len(shards) > 0:
        array = level_of(rng, extent, shards, -0.22, 0.18) * array
    return jnp.clip(array, min=-limit, max=limit).astype(held_as)


def setup_inputs(seed: int = 0) -> dict:
    key_list = jax.random.split(jax.random.key(seed), 4)
    return {
        "blocks": draw_blocks(jax.random.fold_in(key_list[3], 71), 0),
        "col_index": draw_col_index(jax.random.fold_in(key_list[3], 71), 0),
        "vectors": scatter_about(key_list[2], (NORB, STATES), 1.0, 6.0, ((0, 32),), jnp.float32),
    }


LOWER = -2.0
CUTOFF = 0.0
UPPER = 2.0

def filter_coefs(degree):
    half_width = (UPPER - CUTOFF) / 2.0
    center = (UPPER + CUTOFF) / 2.0
    sigma_now = half_width / (LOWER - center)
    tau_value = 2.0 / sigma_now
    scales = [sigma_now / half_width]
    carries = [0.0]
    for number in range(1, degree):
        sigma_next = 1.0 / (tau_value - sigma_now)
        scales.append(2.0 * sigma_next / half_width)
        carries.append(sigma_now * sigma_next)
        sigma_now = sigma_next
    return (center, scales, carries)

def shifted_image(blocks, col_index, lowered, center):
    blocked = lowered.reshape(NBLK, BLOCK, STATES)

    def add_slot(summed, slot_number):
        columns = lax.dynamic_index_in_dim(col_index, slot_number, 1, False)
        block_col = lax.dynamic_index_in_dim(blocks, slot_number, 1, False).astype(jnp.float32)
        picked = blocked[jnp.maximum(columns, 0)].astype(jnp.float32)
        product = jnp.einsum('iab,ibk->iak', block_col, picked)
        return (summed + jnp.where((columns >= 0)[:, None, None], product, 0.0), None)
    initial = jnp.zeros((NBLK, BLOCK, STATES), jnp.float32)
    summed, unused = lax.scan(add_slot, initial, jnp.arange(N_COL * SLOTS, dtype=jnp.int32))
    return summed.reshape(NORB, STATES) - center * lowered.astype(jnp.float32)

def orthonormalize(filtered):
    gram_sum = jnp.dot(filtered.T.astype(jnp.float32), filtered.astype(jnp.float32), precision=lax.Precision.HIGHEST, preferred_element_type=jnp.float32)
    factor = jnp.linalg.cholesky(gram_sum)
    inverse = jax.scipy.linalg.solve_triangular(factor, jnp.eye(STATES, dtype=jnp.float32), lower=True)
    return jnp.dot(filtered.astype(jnp.float32), inverse.T.astype(jnp.float32), precision=lax.Precision.HIGHEST, preferred_element_type=jnp.float32)

def reference(blocks, col_index, vectors):
    center, scales, carries = filter_coefs(DEGREE)
    previous = vectors
    current = vectors
    for number in range(DEGREE):
        summed_image = shifted_image(blocks, col_index, current.astype(jnp.bfloat16), center)
        if number == 0:
            following = scales[0] * summed_image
        else:
            following = scales[number] * summed_image - carries[number] * previous
        previous, current = (current, following)
    return math.sqrt(NORB) * orthonormalize(current)
```

```python
import math

import jax
import jax.numpy as jnp
from jax import lax
from jax.experimental import pallas as pl
from jax.experimental.pallas import tpu as pltpu
from jax.sharding import PartitionSpec as P

DEGREE = 4


LOWER = -2.0
CUTOFF = 0.0
UPPER = 2.0


def filter_coefs(degree):
    half_width = (UPPER - CUTOFF) / 2.0
    center = (UPPER + CUTOFF) / 2.0
    sigma_now = half_width / (LOWER - center)
    tau_value = 2.0 / sigma_now
    scales = [sigma_now / half_width]
    carries = [0.0]
    for number in range(1, degree):
        sigma_next = 1.0 / (tau_value - sigma_now)
        scales.append(2.0 * sigma_next / half_width)
        carries.append(sigma_now * sigma_next)
        sigma_now = sigma_next
    return (center, scales, carries)


def swap(value, axis, distance):
    count = lax.axis_size(axis)
    return lax.ppermute(value, axis, [(i, i ^ distance) for i in range(count)])


def bits_below(count):
    return [1 << n for n in range(count.bit_length() - 1)]


def densify(blocks, col_index, tile_blocks):
    group_rows, slots, width, _ = blocks.shape

    def kernel(index_ref, blocks_ref, tile_ref):
        row = pl.program_id(0)
        tile_ref[...] = jnp.zeros_like(tile_ref)
        for slot in range(slots):
            place = index_ref[row, slot]

            @pl.when(place >= 0)
            def _():
                start = pl.multiple_of(lax.rem(place, tile_blocks) * width, width)
                tile_ref[:, pl.ds(start, width)] = blocks_ref[0, slot]

    return pl.pallas_call(
        kernel,
        grid_spec=pltpu.PrefetchScalarGridSpec(
            num_scalar_prefetch=1,
            grid=(group_rows,),
            in_specs=[pl.BlockSpec((1, slots, width, width), lambda i, index: (i, 0, 0, 0))],
            out_specs=pl.BlockSpec((width, tile_blocks * width), lambda i, index: (i, 0)),
        ),
        out_shape=jax.ShapeDtypeStruct((group_rows * width, tile_blocks * width), blocks.dtype),
    )(col_index, blocks)


def exact_dot(a, b, dims):
    return lax.dot_general(
        a, b, (dims, ((), ())), precision=lax.Precision.HIGHEST, preferred_element_type=jnp.float32
    )


def factor_in_place(ref, size):
    rows = lax.broadcasted_iota(jnp.int32, (size, size), 0)
    lanes = lax.broadcasted_iota(jnp.int32, (size, size), 1)
    lane_row = lax.broadcasted_iota(jnp.int32, (1, size), 1)

    def pivot(j, unused):
        row = ref[pl.ds(j, 1), :]
        here = lane_row == j
        d = jnp.sum(jnp.where(here, row, 0.0), axis=1, keepdims=True)
        inv_root = lax.rsqrt(d)
        inv = 1.0 / d
        matrix = ref[...]
        below = rows > j
        column = jnp.sum(jnp.where(lanes == j, matrix, 0.0), axis=1, keepdims=True)
        pivot_row = jnp.where(here, 1.0, row)
        scaled = pivot_row * inv
        kept = jnp.where((lanes == j) & below, 0.0, matrix)
        ref[...] = kept - jnp.where(below, column * scaled, 0.0)
        ref[pl.ds(j, 1), :] = pivot_row * inv_root
        return unused

    lax.fori_loop(0, size, pivot, 0)


def inverse_factor(cross, packed):
    size = cross.shape[0]

    def kernel(cross_ref, packed_ref, out_ref, work):
        rows = lax.broadcasted_iota(jnp.int32, (size, size), 0)
        lanes = lax.broadcasted_iota(jnp.int32, (size, size), 1)
        both = packed_ref[:size, :]
        mirrored = both.T
        work[...] = jnp.where(rows >= lanes, both, mirrored)
        factor_in_place(work, size)
        first = jnp.where(rows >= lanes, work[...], 0.0)
        below = exact_dot(cross_ref[...], first, ((1,), (1,)))
        second = jnp.where(lanes > rows, both, mirrored)
        second = jnp.where(lanes == rows, packed_ref[size : size + 1, :], second)
        work[...] = second - exact_dot(below, below, ((1,), (1,)))
        factor_in_place(work, size)
        last = jnp.where(rows >= lanes, work[...], 0.0)
        out_ref[:size, :size] = first
        out_ref[:size, size:] = jnp.zeros((size, size), jnp.float32)
        out_ref[size:, :size] = -exact_dot(
            last, exact_dot(below, first, ((1,), (0,))), ((1,), (0,))
        )
        out_ref[size:, size:] = last

    return pl.pallas_call(
        kernel,
        out_shape=jax.ShapeDtypeStruct((2 * size, 2 * size), jnp.float32),
        scratch_shapes=[pltpu.VMEM((size, size), jnp.float32)],
    )(cross, packed)


def on_device(blocks, col_index, vectors):
    center, scales, carries = filter_coefs(DEGREE)
    row_count = lax.axis_size("row")
    col_count = lax.axis_size("col")
    row_rank = lax.axis_index("row")
    col_rank = lax.axis_index("col")
    core = col_rank % 2
    group_rows, _, width, _ = blocks.shape
    piece_rows, states = vectors.shape
    half = states // 2
    tile_blocks = piece_rows // width * row_count
    tile_rows = tile_blocks * width
    row_bits = bits_below(row_count)
    z_bits = [2 * bit for bit in bits_below(col_count // 2)]
    narrow = jnp.bfloat16

    mine_first = core == 0
    left, right = vectors[:, :half], vectors[:, half:]
    own_start = jnp.where(mine_first, left, right)
    other_start = swap(jnp.where(mine_first, right, left), "col", 1)
    start = jnp.stack([own_start, other_start])
    low_start = start.astype(narrow)

    arrived = [low_start] + [swap(low_start, "row", k) for k in range(1, row_count)]
    arrived = jnp.stack(arrived)
    ordered = jnp.stack([lax.dynamic_index_in_dim(arrived, row_rank ^ k, 0, False) for k in range(row_count)])
    low_own = ordered[:, 0].reshape(tile_rows, half)
    low_other = ordered[:, 1].reshape(tile_rows, half)

    own = densify(blocks, col_index, tile_blocks)
    other = swap(own, "col", 1)

    first_row = row_rank * group_rows
    own_offset = first_row - col_rank * tile_blocks
    other_offset = first_row - (col_rank ^ 1) * tile_blocks

    def rows_from(value, offset, value_blocks, wanted_blocks):
        edge = jnp.zeros((wanted_blocks * width, value.shape[1]), value.dtype)
        padded = jnp.concatenate([edge, value, edge])
        begin = jnp.clip(offset + wanted_blocks, 0, value_blocks + wanted_blocks)
        return lax.dynamic_slice_in_dim(padded, begin * width, wanted_blocks * width, 0)

    def forward(low_own, low_other):
        product = jnp.dot(own, low_own, preferred_element_type=jnp.float32)
        product = product + jnp.dot(other, low_other, preferred_element_type=jnp.float32)
        diagonal = rows_from(low_own, own_offset, tile_blocks, group_rows).astype(jnp.float32)
        diagonal += rows_from(low_other, other_offset, tile_blocks, group_rows).astype(jnp.float32)
        return product - center * diagonal

    def backward(low):
        def part(tile, offset):
            product = lax.dot_general(tile, low, (((0,), (0,)), ((), ())), preferred_element_type=jnp.float32)
            diagonal = rows_from(low, -offset, group_rows, tile_blocks).astype(jnp.float32)
            return product - center * diagonal

        return part(own, own_offset), part(other, other_offset)

    def halves_of(value, bit):
        rows = value.shape[0] // 2
        upper = (col_rank & bit) != 0
        first, second = value[:rows], value[rows:]
        return jnp.where(upper, second, first), jnp.where(upper, first, second)

    def sum_over_z(value):
        for bit in z_bits[:-1]:
            kept, sent = halves_of(value, bit)
            value = kept + swap(sent.astype(narrow), "col", bit).astype(jnp.float32)
        for bit in z_bits[-1:]:
            sent = value.astype(narrow)
            value = sent.astype(jnp.float32) + swap(sent, "col", bit).astype(jnp.float32)
        return value

    def gather_over_z(value):
        for bit in reversed(z_bits[:-1]):
            partner = swap(value, "col", bit)
            upper = (col_rank & bit) != 0
            value = jnp.concatenate(
                [jnp.where(upper, partner, value), jnp.where(upper, value, partner)]
            )
        return value

    def sum_over_row(one, two):
        for bit_one, bit_two in zip(row_bits, reversed(row_bits)):
            one, two = one + swap(one, "row", bit_one), two + swap(two, "row", bit_two)
        return one, two

    def placed(piece):
        here = jnp.arange(row_count)[:, None, None] == row_rank
        return jnp.where(here, piece[None], 0.0).reshape(tile_rows, half)

    y1 = scales[0] * sum_over_z(forward(low_own, low_other))
    low = gather_over_z(y1.astype(narrow))
    part_own, part_other = backward(low)
    y2_own, y2_other = sum_over_row(
        scales[1] * part_own - carries[1] * placed(start[0]),
        scales[1] * part_other - carries[1] * placed(start[1]),
    )
    y3 = scales[2] * sum_over_z(forward(y2_own.astype(narrow), y2_other.astype(narrow))) - carries[2] * y1
    low = gather_over_z(y3.astype(narrow))
    part_own, part_other = backward(low)
    image_own, image_other = sum_over_row(part_own, part_other)
    y4_own = scales[3] * image_own - carries[3] * y2_own
    y4_other = scales[3] * image_other - carries[3] * y2_other

    partner = swap(y4_other, "col", 1)
    filtered = jnp.concatenate(
        [jnp.where(mine_first, y4_own, partner), jnp.where(mine_first, partner, y4_own)], axis=1
    )
    gram = exact_dot(filtered, filtered, ((0,), (0,)))
    rows = lax.broadcasted_iota(jnp.int32, (half, half), 0)
    lanes = lax.broadcasted_iota(jnp.int32, (half, half), 1)
    corner = gram[half:, half:]
    cross = gram[half:, :half]
    packed = jnp.where(rows >= lanes, gram[:half, :half], corner)
    diagonal = jnp.sum(jnp.where(rows == lanes, corner, 0.0), axis=0, keepdims=True)
    cross = jnp.pad(cross, ((0, 8), (0, 0)))
    packed = jnp.concatenate([packed, diagonal, jnp.zeros((7, half), jnp.float32)])
    total = jnp.where(mine_first, cross, packed) + swap(jnp.where(mine_first, packed, cross), "col", 1)
    for bit in z_bits:
        total = total + swap(total, "col", bit)
    partner = swap(total, "col", 1)
    cross = jnp.where(mine_first, total, partner)[:half]
    packed = jnp.where(mine_first, partner, total)
    inverse = inverse_factor(cross, packed)

    mine = lax.dynamic_slice_in_dim(filtered, row_rank * piece_rows, piece_rows, 0)
    orbital_count = piece_rows * row_count * col_count
    return math.sqrt(orbital_count) * exact_dot(mine, inverse, ((1,), (1,)))


def solution(mesh):
    return jax.shard_map(
        on_device,
        mesh=mesh,
        in_specs=(P("row", "col", None, None), P("row", "col"), P(("col", "row"), None)),
        out_specs=P(("col", "row"), None),
        check_vma=False,
    )
```

```python
import math

import jax
import jax.numpy as jnp
from jax import lax
from jax.experimental import pallas as pl
from jax.experimental.pallas import tpu as pltpu
from jax.sharding import PartitionSpec as P

DEGREE = 4


LOWER = -2.0
CUTOFF = 0.0
UPPER = 2.0


def filter_coefs(degree):
    half_width = (UPPER - CUTOFF) / 2.0
    center = (UPPER + CUTOFF) / 2.0
    sigma_now = half_width / (LOWER - center)
    tau_value = 2.0 / sigma_now
    scales = [sigma_now / half_width]
    carries = [0.0]
    for number in range(1, degree):
        sigma_next = 1.0 / (tau_value - sigma_now)
        scales.append(2.0 * sigma_next / half_width)
        carries.append(sigma_now * sigma_next)
        sigma_now = sigma_next
    return (center, scales, carries)


def swap(value, axis, distance):
    count = lax.axis_size(axis)
    return lax.ppermute(value, axis, [(i, i ^ distance) for i in range(count)])


def bits_below(count):
    return [1 << n for n in range(count.bit_length() - 1)]


def densify(blocks, col_index, tile_blocks):
    group_rows, slots, width, _ = blocks.shape
    slots = min(slots, tile_blocks)
    step = 2

    def kernel(index_ref, blocks_ref, tile_ref):
        nothing = jnp.zeros((width, width), blocks.dtype)
        for inner in range(step):
            places = [index_ref[pl.program_id(0) * step + inner, slot] for slot in range(slots)]
            places = [jnp.where(place >= 0, lax.rem(place, tile_blocks), -1) for place in places]
            for column in range(tile_blocks):
                value = nothing
                for slot in range(slots):
                    value = jnp.where(places[slot] == column, blocks_ref[inner, slot], value)
                tile_ref[inner * width : (inner + 1) * width, column * width : (column + 1) * width] = value

    return pl.pallas_call(
        kernel,
        grid_spec=pltpu.PrefetchScalarGridSpec(
            num_scalar_prefetch=1,
            grid=(group_rows // step,),
            in_specs=[pl.BlockSpec((step, slots, width, width), lambda i, index: (i, 0, 0, 0))],
            out_specs=pl.BlockSpec((step * width, tile_blocks * width), lambda i, index: (i, 0)),
        ),
        out_shape=jax.ShapeDtypeStruct((group_rows * width, tile_blocks * width), blocks.dtype),
    )(col_index, blocks)


def exact_dot(a, b, dims):
    return lax.dot_general(
        a, b, (dims, ((), ())), precision=lax.Precision.HIGHEST, preferred_element_type=jnp.float32
    )


def factor(matrix, tall):
    size = matrix.shape[1]
    groups = [matrix[first : first + tall] for first in range(0, size, tall)]
    sub = lax.broadcasted_iota(jnp.int32, (tall, size), 0)
    lane = lax.broadcasted_iota(jnp.int32, (tall, size), 1)
    for number, head in enumerate(groups):
        first = tall * number
        block = (lane >= first) & (lane < first + tall)
        columns = [jnp.broadcast_to(head[:, first + q : first + q + 1], head.shape) for q in range(tall)]
        x = jnp.where(block, jnp.where(lane - first == sub, 1.0, 0.0), head)
        z = x
        pivots = jnp.ones_like(x)
        inverses = jnp.ones_like(x)
        for p in range(tall):
            pivot = columns[p][p : p + 1, :]
            inverse = 1.0 / pivot
            ratio = columns[p] * inverse
            below = jnp.where(sub > p, ratio, 0.0)
            others = jnp.where(sub == p, 0.0, ratio)
            for q in range(p + 1, tall):
                columns[q] = columns[q] - others * columns[q][p : p + 1, :]
            x = x - below * x[p : p + 1, :]
            z = z - others * z[p : p + 1, :]
            pivots = jnp.where(sub == p, pivot, pivots)
            inverses = jnp.where(sub == p, inverse, inverses)
        z = z * inverses
        for later in range(number + 1, len(groups)):
            value = jnp.where(block, 0.0, groups[later])
            for p in range(tall):
                value = value - groups[later][:, first + p : first + p + 1] * z[p : p + 1, :]
            groups[later] = value
        groups[number] = x * lax.rsqrt(pivots)
    return jnp.concatenate(groups)


def orthonormal(total, partner, filtered, mine_first, scale):
    size = total.shape[1]
    tall = 16

    def kernel(first_ref, total_ref, partner_ref, filtered_ref, out_ref):
        rows = lax.broadcasted_iota(jnp.int32, (size, size), 0)
        lanes = lax.broadcasted_iota(jnp.int32, (size, size), 1)
        is_first = first_ref[0] != 0
        cross = jnp.where(is_first, total_ref[:size, :], partner_ref[:size, :])
        both = jnp.where(is_first, partner_ref[:size, :], total_ref[:size, :])
        diagonal = jnp.where(is_first, partner_ref[size : size + 1, :], total_ref[size : size + 1, :])
        mirrored = both.T
        first = factor(jnp.where(rows >= lanes, both, mirrored), tall)
        first = jnp.where(rows >= lanes, first, 0.0)
        below = exact_dot(cross, first, ((1,), (1,)))
        second = jnp.where(lanes > rows, both, mirrored)
        second = jnp.where(lanes == rows, diagonal, second)
        last = factor(second - exact_dot(below, below, ((1,), (1,))), tall)
        last = jnp.where(rows >= lanes, last, 0.0)
        left = exact_dot(filtered_ref[:, :size], first, ((1,), (1,)))
        out_ref[:, :size] = scale * left
        right = filtered_ref[:, size:] - exact_dot(left, below, ((1,), (1,)))
        out_ref[:, size:] = scale * exact_dot(right, last, ((1,), (1,)))

    return pl.pallas_call(
        kernel,
        grid_spec=pltpu.PrefetchScalarGridSpec(
            num_scalar_prefetch=1,
            grid=(1,),
            in_specs=[pl.BlockSpec(a.shape, lambda i, first: (0, 0)) for a in (total, partner, filtered)],
            out_specs=pl.BlockSpec(filtered.shape, lambda i, first: (0, 0)),
        ),
        out_shape=jax.ShapeDtypeStruct(filtered.shape, jnp.float32),
    )(mine_first.astype(jnp.int32).reshape(1), total, partner, filtered)


def on_device(blocks, col_index, vectors):
    center, scales, carries = filter_coefs(DEGREE)
    row_count = lax.axis_size("row")
    col_count = lax.axis_size("col")
    row_rank = lax.axis_index("row")
    col_rank = lax.axis_index("col")
    core = col_rank % 2
    group_rows, _, width, _ = blocks.shape
    piece_rows, states = vectors.shape
    half = states // 2
    tile_blocks = piece_rows // width * row_count
    tile_rows = tile_blocks * width
    row_bits = bits_below(row_count)
    z_bits = [2 * bit for bit in bits_below(col_count // 2)]
    narrow = jnp.bfloat16

    mine_first = core == 0
    left, right = vectors[:, :half], vectors[:, half:]
    own_start = jnp.where(mine_first, left, right)
    other_start = swap(jnp.where(mine_first, right, left), "col", 1)
    start = jnp.stack([own_start, other_start])
    low_start = start.astype(narrow)

    arrived = [low_start] + [swap(low_start, "row", k) for k in range(1, row_count)]
    arrived = jnp.stack(arrived)
    ordered = jnp.stack([lax.dynamic_index_in_dim(arrived, row_rank ^ k, 0, False) for k in range(row_count)])
    low_own = ordered[:, 0].reshape(tile_rows, half)
    low_other = ordered[:, 1].reshape(tile_rows, half)

    own = densify(blocks, col_index, tile_blocks)
    other = swap(own, "col", 1)

    first_row = row_rank * group_rows
    own_offset = first_row - col_rank * tile_blocks
    other_offset = first_row - (col_rank ^ 1) * tile_blocks

    segments = group_rows // tile_blocks

    def spread(low, offset):
        value = low.astype(jnp.float32)
        return jnp.concatenate(
            [jnp.where(offset == -k * tile_blocks, value, 0.0) for k in range(segments)]
        )

    def picked(low, offset):
        value = low.astype(jnp.float32).reshape(segments, tile_rows, half)
        parts = [jnp.where(offset == -k * tile_blocks, value[k], 0.0) for k in range(segments)]
        return sum(parts[1:], parts[0])

    def forward(low_own, low_other):
        product = jnp.dot(own, low_own, preferred_element_type=jnp.float32)
        product = product + jnp.dot(other, low_other, preferred_element_type=jnp.float32)
        return product - center * (spread(low_own, own_offset) + spread(low_other, other_offset))

    def backward(low):
        def part(tile, offset):
            product = lax.dot_general(tile, low, (((0,), (0,)), ((), ())), preferred_element_type=jnp.float32)
            return product - center * picked(low, offset)

        return part(own, own_offset), part(other, other_offset)

    def halves_of(value, bit):
        rows = value.shape[0] // 2
        upper = (col_rank & bit) != 0
        first, second = value[:rows], value[rows:]
        return jnp.where(upper, second, first), jnp.where(upper, first, second)

    def sum_over_z(value):
        for bit in z_bits[:-1]:
            kept, sent = halves_of(value, bit)
            value = kept + swap(sent.astype(narrow), "col", bit).astype(jnp.float32)
        for bit in z_bits[-1:]:
            sent = value.astype(narrow)
            value = sent.astype(jnp.float32) + swap(sent, "col", bit).astype(jnp.float32)
        return value

    def gather_over_z(value):
        for bit in reversed(z_bits[:-1]):
            partner = swap(value, "col", bit)
            upper = (col_rank & bit) != 0
            value = jnp.concatenate(
                [jnp.where(upper, partner, value), jnp.where(upper, value, partner)]
            )
        return value

    def sum_over_row(one, two):
        for bit_one, bit_two in zip(row_bits, reversed(row_bits)):
            one, two = one + swap(one, "row", bit_one), two + swap(two, "row", bit_two)
        return one, two

    def placed(piece):
        here = jnp.arange(row_count)[:, None, None] == row_rank
        return jnp.where(here, piece[None], 0.0).reshape(tile_rows, half)

    y1 = scales[0] * sum_over_z(forward(low_own, low_other))
    low = gather_over_z(y1.astype(narrow))
    part_own, part_other = backward(low)
    y2_own, y2_other = sum_over_row(
        scales[1] * part_own - carries[1] * placed(start[0]),
        scales[1] * part_other - carries[1] * placed(start[1]),
    )
    y3 = scales[2] * sum_over_z(forward(y2_own.astype(narrow), y2_other.astype(narrow))) - carries[2] * y1
    low = gather_over_z(y3.astype(narrow))
    part_own, part_other = backward(low)
    image_own, image_other = sum_over_row(part_own, part_other)
    y4_own = scales[3] * image_own - carries[3] * y2_own
    y4_other = scales[3] * image_other - carries[3] * y2_other

    partner = swap(y4_other, "col", 1)
    filtered = jnp.concatenate(
        [jnp.where(mine_first, y4_own, partner), jnp.where(mine_first, partner, y4_own)], axis=1
    )
    gram = exact_dot(filtered, filtered, ((0,), (0,)))
    rows = lax.broadcasted_iota(jnp.int32, (half, half), 0)
    lanes = lax.broadcasted_iota(jnp.int32, (half, half), 1)
    corner = gram[half:, half:]
    cross = gram[half:, :half]
    packed = jnp.where(rows >= lanes, gram[:half, :half], corner)
    diagonal = jnp.sum(jnp.where(rows == lanes, corner, 0.0), axis=0, keepdims=True)
    cross = jnp.pad(cross, ((0, 8), (0, 0)))
    packed = jnp.concatenate([packed, diagonal, jnp.zeros((7, half), jnp.float32)])
    total = jnp.where(mine_first, cross, packed) + swap(jnp.where(mine_first, packed, cross), "col", 1)
    for bit in z_bits:
        total = total + swap(total, "col", bit)
    partner = swap(total, "col", 1)
    mine = lax.dynamic_slice_in_dim(filtered, row_rank * piece_rows, piece_rows, 0)
    orbital_count = piece_rows * row_count * col_count
    return orthonormal(total, partner, mine, mine_first, math.sqrt(orbital_count))


def solution(mesh):
    return jax.shard_map(
        on_device,
        mesh=mesh,
        in_specs=(P("row", "col", None, None), P("row", "col"), P(("col", "row"), None)),
        out_specs=P(("col", "row"), None),
        check_vma=False,
    )
```

```python
import math

import jax
import jax.numpy as jnp
from jax import lax
from jax.experimental import pallas as pl
from jax.experimental.pallas import tpu as pltpu
from jax.sharding import PartitionSpec as P

DEGREE = 4


LOWER = -2.0
CUTOFF = 0.0
UPPER = 2.0


def filter_coefs(degree):
    half_width = (UPPER - CUTOFF) / 2.0
    center = (UPPER + CUTOFF) / 2.0
    sigma_now = half_width / (LOWER - center)
    tau_value = 2.0 / sigma_now
    scales = [sigma_now / half_width]
    carries = [0.0]
    for number in range(1, degree):
        sigma_next = 1.0 / (tau_value - sigma_now)
        scales.append(2.0 * sigma_next / half_width)
        carries.append(sigma_now * sigma_next)
        sigma_now = sigma_next
    return (center, scales, carries)


def swap(value, axis, distance):
    count = lax.axis_size(axis)
    return lax.ppermute(value, axis, [(i, i ^ distance) for i in range(count)])


def bits_below(count):
    return [1 << n for n in range(count.bit_length() - 1)]


def in_order(values, rank):
    stacked = jnp.stack(values)
    return jnp.concatenate(
        [lax.dynamic_index_in_dim(stacked, rank ^ k, 0, False) for k in range(len(values))]
    )


def densify(blocks, col_index, tile_blocks):
    group_rows, slots, width, _ = blocks.shape
    slots = min(slots, tile_blocks)
    step = max(group_rows // 2, 1)

    def kernel(index_ref, blocks_ref, tile_ref):
        nothing = jnp.zeros((width, width), blocks.dtype)
        for inner in range(step):
            places = [index_ref[pl.program_id(0) * step + inner, slot] for slot in range(slots)]
            places = [jnp.where(place >= 0, lax.rem(place, tile_blocks), -1) for place in places]
            for column in range(tile_blocks):
                value = nothing
                for slot in range(slots):
                    value = jnp.where(places[slot] == column, blocks_ref[inner, slot], value)
                tile_ref[inner * width : (inner + 1) * width, column * width : (column + 1) * width] = value

    return pl.pallas_call(
        kernel,
        grid_spec=pltpu.PrefetchScalarGridSpec(
            num_scalar_prefetch=1,
            grid=(group_rows // step,),
            in_specs=[pl.BlockSpec((step, slots, width, width), lambda i, index: (i, 0, 0, 0))],
            out_specs=pl.BlockSpec((step * width, tile_blocks * width), lambda i, index: (i, 0)),
        ),
        out_shape=jax.ShapeDtypeStruct((group_rows * width, tile_blocks * width), blocks.dtype),
    )(col_index, blocks)


def exact_dot(a, b, dims):
    return lax.dot_general(
        a, b, (dims, ((), ())), precision=lax.Precision.HIGHEST, preferred_element_type=jnp.float32
    )


def factor(matrix, tall):
    size = matrix.shape[1]
    groups = [matrix[first : first + tall] for first in range(0, size, tall)]
    sub = lax.broadcasted_iota(jnp.int32, (tall, size), 0)
    lane = lax.broadcasted_iota(jnp.int32, (tall, size), 1)
    for number, head in enumerate(groups):
        first = tall * number
        block = (lane >= first) & (lane < first + tall)
        columns = [jnp.broadcast_to(head[:, first + q : first + q + 1], head.shape) for q in range(tall)]
        x = jnp.where(block, jnp.where(lane - first == sub, 1.0, 0.0), head)
        z = x
        pivots = jnp.ones_like(x)
        inverses = jnp.ones_like(x)
        for p in range(tall):
            pivot = columns[p][p : p + 1, :]
            inverse = 1.0 / pivot
            ratio = columns[p] * inverse
            below = jnp.where(sub > p, ratio, 0.0)
            others = jnp.where(sub == p, 0.0, ratio)
            for q in range(p + 1, tall):
                columns[q] = columns[q] - others * columns[q][p : p + 1, :]
            x = x - below * x[p : p + 1, :]
            z = z - others * z[p : p + 1, :]
            pivots = jnp.where(sub == p, pivot, pivots)
            inverses = jnp.where(sub == p, inverse, inverses)
        z = z * inverses
        for later in range(number + 1, len(groups)):
            value = jnp.where(block, 0.0, groups[later])
            for p in range(tall):
                value = value - groups[later][:, first + p : first + p + 1] * z[p : p + 1, :]
            groups[later] = value
        groups[number] = x * lax.rsqrt(pivots)
    return jnp.concatenate(groups)


def orthonormal(total, partner, filtered, mine_first, scale):
    size = total.shape[1]
    tall = 16

    def kernel(first_ref, total_ref, partner_ref, filtered_ref, out_ref):
        rows = lax.broadcasted_iota(jnp.int32, (size, size), 0)
        lanes = lax.broadcasted_iota(jnp.int32, (size, size), 1)
        is_first = first_ref[0] != 0
        cross = jnp.where(is_first, total_ref[:size, :], partner_ref[:size, :])
        both = jnp.where(is_first, partner_ref[:size, :], total_ref[:size, :])
        diagonal = jnp.where(is_first, partner_ref[size : size + 1, :], total_ref[size : size + 1, :])
        mirrored = both.T
        first = factor(jnp.where(rows >= lanes, both, mirrored), tall)
        first = jnp.where(rows >= lanes, first, 0.0)
        below = exact_dot(cross, first, ((1,), (1,)))
        second = jnp.where(lanes > rows, both, mirrored)
        second = jnp.where(lanes == rows, diagonal, second)
        last = factor(second - exact_dot(below, below, ((1,), (1,))), tall)
        last = jnp.where(rows >= lanes, last, 0.0)
        left = exact_dot(filtered_ref[:, :size], first, ((1,), (1,)))
        out_ref[:, :size] = scale * left
        right = filtered_ref[:, size:] - exact_dot(left, below, ((1,), (1,)))
        out_ref[:, size:] = scale * exact_dot(right, last, ((1,), (1,)))

    return pl.pallas_call(
        kernel,
        grid_spec=pltpu.PrefetchScalarGridSpec(
            num_scalar_prefetch=1,
            grid=(1,),
            in_specs=[pl.BlockSpec(a.shape, lambda i, first: (0, 0)) for a in (total, partner, filtered)],
            out_specs=pl.BlockSpec(filtered.shape, lambda i, first: (0, 0)),
        ),
        out_shape=jax.ShapeDtypeStruct(filtered.shape, jnp.float32),
    )(mine_first.astype(jnp.int32).reshape(1), total, partner, filtered)


def on_device(blocks, col_index, vectors):
    center, scales, carries = filter_coefs(DEGREE)
    row_count = lax.axis_size("row")
    col_count = lax.axis_size("col")
    row_rank = lax.axis_index("row")
    col_rank = lax.axis_index("col")
    core = col_rank % 2
    group_rows, _, width, _ = blocks.shape
    piece_rows, states = vectors.shape
    half = states // 2
    tile_blocks = piece_rows // width * row_count
    tile_rows = tile_blocks * width
    row_bits = bits_below(row_count)
    z_count = col_count // 2
    z_rank = col_rank // 2
    z_bits = [2 * bit for bit in bits_below(z_count)]
    narrow = jnp.bfloat16

    mine_first = core == 0
    left, right = vectors[:, :half], vectors[:, half:]
    own_start = jnp.where(mine_first, left, right)
    other_start = swap(jnp.where(mine_first, right, left), "col", 1)
    start = jnp.stack([own_start, other_start])
    low_start = start.astype(narrow)

    arrived = [low_start] + [swap(low_start, "row", k) for k in range(1, row_count)]
    low_own = in_order([value[0] for value in arrived], row_rank)
    low_other = in_order([value[1] for value in arrived], row_rank)

    own = densify(blocks, col_index, tile_blocks)
    other = swap(own, "col", 1)

    first_row = row_rank * group_rows
    own_offset = first_row - col_rank * tile_blocks
    other_offset = first_row - (col_rank ^ 1) * tile_blocks

    segments = group_rows // tile_blocks

    def spread(low, offset):
        value = low.astype(jnp.float32)
        return jnp.concatenate(
            [jnp.where(offset == -k * tile_blocks, value, 0.0) for k in range(segments)]
        )

    def picked(low, offset):
        value = low.astype(jnp.float32).reshape(segments, tile_rows, half)
        parts = [jnp.where(offset == -k * tile_blocks, value[k], 0.0) for k in range(segments)]
        return sum(parts[1:], parts[0])

    def forward(low_own, low_other):
        product = jnp.dot(own, low_own, preferred_element_type=jnp.float32)
        product = product + jnp.dot(other, low_other, preferred_element_type=jnp.float32)
        return product - center * (spread(low_own, own_offset) + spread(low_other, other_offset))

    def backward(low):
        def part(tile, offset):
            product = lax.dot_general(tile, low, (((0,), (0,)), ((), ())), preferred_element_type=jnp.float32)
            return product - center * picked(low, offset)

        return part(own, own_offset), part(other, other_offset)

    def piece_of(value, index):
        rows = value.shape[0] // z_count
        return lax.dynamic_slice_in_dim(value, index * rows, rows, 0)

    def sum_over_z(value):
        sent = value.astype(narrow)
        total = piece_of(value, z_rank)
        for k in range(1, z_count):
            total = total + swap(piece_of(sent, z_rank ^ k), "col", 2 * k).astype(jnp.float32)
        return total

    def gather_over_z(value):
        return in_order([value] + [swap(value, "col", 2 * k) for k in range(1, z_count)], z_rank)

    def sum_over_row(one, two):
        for level, (bit_one, bit_two) in enumerate(zip(row_bits, reversed(row_bits))):
            sent = narrow if level < 2 else jnp.float32
            low_one, low_two = one.astype(sent), two.astype(sent)
            one = low_one.astype(jnp.float32) + swap(low_one, "row", bit_one).astype(jnp.float32)
            two = low_two.astype(jnp.float32) + swap(low_two, "row", bit_two).astype(jnp.float32)
        return one, two

    def placed(piece):
        here = jnp.arange(row_count)[:, None, None] == row_rank
        return jnp.where(here, piece[None], 0.0).reshape(tile_rows, half)

    y1 = scales[0] * sum_over_z(forward(low_own, low_other))
    low = gather_over_z(y1.astype(narrow))
    part_own, part_other = backward(low)
    y2_own, y2_other = sum_over_row(
        scales[1] * part_own - carries[1] * placed(start[0]),
        scales[1] * part_other - carries[1] * placed(start[1]),
    )
    y3 = scales[2] * sum_over_z(forward(y2_own.astype(narrow), y2_other.astype(narrow))) - carries[2] * y1
    low = gather_over_z(y3.astype(narrow))
    part_own, part_other = backward(low)
    image_own, image_other = sum_over_row(part_own, part_other)
    y4_own = scales[3] * image_own - carries[3] * y2_own
    y4_other = scales[3] * image_other - carries[3] * y2_other

    partner = swap(y4_other, "col", 1)
    filtered = jnp.concatenate(
        [jnp.where(mine_first, y4_own, partner), jnp.where(mine_first, partner, y4_own)], axis=1
    )
    gram = exact_dot(filtered, filtered, ((0,), (0,)))
    rows = lax.broadcasted_iota(jnp.int32, (half, half), 0)
    lanes = lax.broadcasted_iota(jnp.int32, (half, half), 1)
    corner = gram[half:, half:]
    cross = gram[half:, :half]
    packed = jnp.where(rows >= lanes, gram[:half, :half], corner)
    diagonal = jnp.sum(jnp.where(rows == lanes, corner, 0.0), axis=0, keepdims=True)
    cross = jnp.pad(cross, ((0, 8), (0, 0)))
    packed = jnp.concatenate([packed, diagonal, jnp.zeros((7, half), jnp.float32)])
    total = jnp.where(mine_first, cross, packed) + swap(jnp.where(mine_first, packed, cross), "col", 1)
    for bit in z_bits:
        total = total + swap(total, "col", bit)
    partner = swap(total, "col", 1)
    mine = lax.dynamic_slice_in_dim(filtered, row_rank * piece_rows, piece_rows, 0)
    orbital_count = piece_rows * row_count * col_count
    return orthonormal(total, partner, mine, mine_first, math.sqrt(orbital_count))


def solution(mesh):
    return jax.shard_map(
        on_device,
        mesh=mesh,
        in_specs=(P("row", "col", None, None), P("row", "col"), P(("col", "row"), None)),
        out_specs=P(("col", "row"), None),
        check_vma=False,
    )
```

```python
import math

import jax
import jax.numpy as jnp
from jax import lax
from jax.experimental import pallas as pl
from jax.experimental.pallas import tpu as pltpu
from jax.sharding import PartitionSpec as P

DEGREE = 4


LOWER = -2.0
CUTOFF = 0.0
UPPER = 2.0


def filter_coefs(degree):
    half_width = (UPPER - CUTOFF) / 2.0
    center = (UPPER + CUTOFF) / 2.0
    sigma_now = half_width / (LOWER - center)
    tau_value = 2.0 / sigma_now
    scales = [sigma_now / half_width]
    carries = [0.0]
    for number in range(1, degree):
        sigma_next = 1.0 / (tau_value - sigma_now)
        scales.append(2.0 * sigma_next / half_width)
        carries.append(sigma_now * sigma_next)
        sigma_now = sigma_next
    return (center, scales, carries)


def swap(value, axis, distance):
    count = lax.axis_size(axis)
    return lax.ppermute(value, axis, [(i, i ^ distance) for i in range(count)])


def bits_below(count):
    return [1 << n for n in range(count.bit_length() - 1)]


def in_order(values, rank):
    stacked = jnp.stack(values)
    return jnp.concatenate(
        [lax.dynamic_index_in_dim(stacked, rank ^ k, 0, False) for k in range(len(values))]
    )


def densify(blocks, col_index, tile_blocks):
    group_rows, slots, width, _ = blocks.shape
    slots = min(slots, tile_blocks)
    step = max(group_rows // 2, 1)

    def kernel(index_ref, blocks_ref, tile_ref):
        nothing = jnp.zeros((width, width), blocks.dtype)
        for inner in range(step):
            places = [index_ref[pl.program_id(0) * step + inner, slot] for slot in range(slots)]
            places = [jnp.where(place >= 0, lax.rem(place, tile_blocks), -1) for place in places]
            for column in range(tile_blocks):
                value = nothing
                for slot in range(slots):
                    value = jnp.where(places[slot] == column, blocks_ref[inner, slot], value)
                tile_ref[inner * width : (inner + 1) * width, column * width : (column + 1) * width] = value

    return pl.pallas_call(
        kernel,
        grid_spec=pltpu.PrefetchScalarGridSpec(
            num_scalar_prefetch=1,
            grid=(group_rows // step,),
            in_specs=[pl.BlockSpec((step, slots, width, width), lambda i, index: (i, 0, 0, 0))],
            out_specs=pl.BlockSpec((step * width, tile_blocks * width), lambda i, index: (i, 0)),
        ),
        out_shape=jax.ShapeDtypeStruct((group_rows * width, tile_blocks * width), blocks.dtype),
    )(col_index, blocks)


def exact_dot(a, b, dims):
    return lax.dot_general(
        a, b, (dims, ((), ())), precision=lax.Precision.HIGHEST, preferred_element_type=jnp.float32
    )


def factor(matrix, tall):
    size = matrix.shape[1]
    groups = [matrix[first : first + tall] for first in range(0, size, tall)]
    sub = lax.broadcasted_iota(jnp.int32, (tall, size), 0)
    lane = lax.broadcasted_iota(jnp.int32, (tall, size), 1)
    for number, head in enumerate(groups):
        first = tall * number
        block = (lane >= first) & (lane < first + tall)
        columns = [jnp.broadcast_to(head[:, first + q : first + q + 1], head.shape) for q in range(tall)]
        x = jnp.where(block, jnp.where(lane - first == sub, 1.0, 0.0), head)
        z = x
        pivots = jnp.ones_like(x)
        inverses = jnp.ones_like(x)
        for p in range(tall):
            pivot = columns[p][p : p + 1, :]
            inverse = 1.0 / pivot
            ratio = columns[p] * inverse
            below = jnp.where(sub > p, ratio, 0.0)
            others = jnp.where(sub == p, 0.0, ratio)
            for q in range(p + 1, tall):
                columns[q] = columns[q] - others * columns[q][p : p + 1, :]
            x = x - below * x[p : p + 1, :]
            z = z - others * z[p : p + 1, :]
            pivots = jnp.where(sub == p, pivot, pivots)
            inverses = jnp.where(sub == p, inverse, inverses)
        z = z * inverses
        for later in range(number + 1, len(groups)):
            value = jnp.where(block, 0.0, groups[later])
            for p in range(tall):
                value = value - groups[later][:, first + p : first + p + 1] * z[p : p + 1, :]
            groups[later] = value
        groups[number] = x * lax.rsqrt(pivots)
    return jnp.concatenate(groups)


def orthonormal(total, partner, filtered, mine_first, rank, piece_rows, scale):
    size = total.shape[1]
    tall = 16

    def kernel(flags_ref, total_ref, partner_ref, filtered_ref, out_ref):
        rows = lax.broadcasted_iota(jnp.int32, (size, size), 0)
        lanes = lax.broadcasted_iota(jnp.int32, (size, size), 1)
        is_first = flags_ref[0] != 0
        start = pl.multiple_of(flags_ref[1] * piece_rows, piece_rows)
        cross = jnp.where(is_first, total_ref[:size, :], partner_ref[:size, :])
        both = jnp.where(is_first, partner_ref[:size, :], total_ref[:size, :])
        diagonal = jnp.where(is_first, partner_ref[size : size + 1, :], total_ref[size : size + 1, :])
        mirrored = both.T
        first = factor(jnp.where(rows >= lanes, both, mirrored), tall)
        first = jnp.where(rows >= lanes, first, 0.0)
        below = exact_dot(cross, first, ((1,), (1,)))
        second = jnp.where(lanes > rows, both, mirrored)
        second = jnp.where(lanes == rows, diagonal, second)
        last = factor(second - exact_dot(below, below, ((1,), (1,))), tall)
        last = jnp.where(rows >= lanes, last, 0.0)
        left = exact_dot(filtered_ref[pl.ds(start, piece_rows), :size], first, ((1,), (1,)))
        out_ref[:, :size] = scale * left
        right = filtered_ref[pl.ds(start, piece_rows), size:] - exact_dot(left, below, ((1,), (1,)))
        out_ref[:, size:] = scale * exact_dot(right, last, ((1,), (1,)))

    vmem = pl.BlockSpec(memory_space=pltpu.VMEM)
    return pl.pallas_call(
        kernel,
        in_specs=[pl.BlockSpec(memory_space=pltpu.SMEM), vmem, vmem, vmem],
        out_specs=vmem,
        out_shape=jax.ShapeDtypeStruct((piece_rows, 2 * size), jnp.float32),
    )(jnp.stack([mine_first.astype(jnp.int32), rank]), total, partner, filtered)


def on_device(blocks, col_index, vectors):
    center, scales, carries = filter_coefs(DEGREE)
    row_count = lax.axis_size("row")
    col_count = lax.axis_size("col")
    row_rank = lax.axis_index("row")
    col_rank = lax.axis_index("col")
    core = col_rank % 2
    group_rows, _, width, _ = blocks.shape
    piece_rows, states = vectors.shape
    half = states // 2
    tile_blocks = piece_rows // width * row_count
    tile_rows = tile_blocks * width
    row_bits = bits_below(row_count)
    z_count = col_count // 2
    z_rank = col_rank // 2
    z_bits = [2 * bit for bit in bits_below(z_count)]
    narrow = jnp.bfloat16

    mine_first = core == 0

    def kept_and_sent(value):
        left, right = value[:, :half], value[:, half:]
        return jnp.where(mine_first, left, right), jnp.where(mine_first, right, left)

    low_start = vectors.astype(narrow)
    arrived = [low_start] + [swap(low_start, "row", k) for k in range(1, row_count)]
    low_own, sent = kept_and_sent(in_order(arrived, row_rank))
    low_other = swap(sent, "col", 1)
    own_start, sent = kept_and_sent(vectors)
    other_start = swap(sent, "col", 1)

    own = densify(blocks, col_index, tile_blocks)
    other = swap(own, "col", 1)

    first_row = row_rank * group_rows
    own_offset = first_row - col_rank * tile_blocks
    other_offset = first_row - (col_rank ^ 1) * tile_blocks

    segments = group_rows // tile_blocks

    def spread(low, offset):
        value = low.astype(jnp.float32)
        return jnp.concatenate(
            [jnp.where(offset == -k * tile_blocks, value, 0.0) for k in range(segments)]
        )

    def picked(low, offset):
        value = low.astype(jnp.float32).reshape(segments, tile_rows, half)
        parts = [jnp.where(offset == -k * tile_blocks, value[k], 0.0) for k in range(segments)]
        return sum(parts[1:], parts[0])

    def forward(low_own, low_other):
        product = jnp.dot(own, low_own, preferred_element_type=jnp.float32)
        product = product + jnp.dot(other, low_other, preferred_element_type=jnp.float32)
        return product - center * (spread(low_own, own_offset) + spread(low_other, other_offset))

    def backward(low):
        def part(tile, offset):
            product = lax.dot_general(tile, low, (((0,), (0,)), ((), ())), preferred_element_type=jnp.float32)
            return product - center * picked(low, offset)

        return part(own, own_offset), part(other, other_offset)

    def piece_of(value, index):
        rows = value.shape[0] // z_count
        return lax.dynamic_slice_in_dim(value, index * rows, rows, 0)

    def sum_over_z(value):
        sent = value.astype(narrow)
        total = piece_of(value, z_rank)
        for k in range(1, z_count):
            total = total + swap(piece_of(sent, z_rank ^ k), "col", 2 * k).astype(jnp.float32)
        return total

    def gather_over_z(value):
        return in_order([value] + [swap(value, "col", 2 * k) for k in range(1, z_count)], z_rank)

    def sum_over_row(one, two):
        for level, (bit_one, bit_two) in enumerate(zip(row_bits, reversed(row_bits))):
            sent = narrow if level < 2 else jnp.float32
            low_one, low_two = lax.optimization_barrier((one.astype(sent), two.astype(sent)))
            from_one, from_two = lax.optimization_barrier(
                (swap(low_one, "row", bit_one), swap(low_two, "row", bit_two))
            )
            one = low_one.astype(jnp.float32) + from_one.astype(jnp.float32)
            two = low_two.astype(jnp.float32) + from_two.astype(jnp.float32)
        return one, two

    def placed(piece):
        here = jnp.arange(row_count)[:, None, None] == row_rank
        return jnp.where(here, piece[None], 0.0).reshape(tile_rows, half)

    y1 = scales[0] * sum_over_z(forward(low_own, low_other))
    low = gather_over_z(y1.astype(narrow))
    part_own, part_other = backward(low)
    y2_own, y2_other = sum_over_row(
        scales[1] * part_own - carries[1] * placed(own_start),
        scales[1] * part_other - carries[1] * placed(other_start),
    )
    y3 = scales[2] * sum_over_z(forward(y2_own.astype(narrow), y2_other.astype(narrow))) - carries[2] * y1
    low = gather_over_z(y3.astype(narrow))
    part_own, part_other = backward(low)
    image_own, image_other = sum_over_row(part_own, part_other)
    y4_own = scales[3] * image_own - carries[3] * y2_own
    y4_other = scales[3] * image_other - carries[3] * y2_other

    partner = swap(y4_other, "col", 1)
    filtered = jnp.concatenate(
        [jnp.where(mine_first, y4_own, partner), jnp.where(mine_first, partner, y4_own)], axis=1
    )
    gram = exact_dot(filtered, filtered, ((0,), (0,)))
    rows = lax.broadcasted_iota(jnp.int32, (half, half), 0)
    lanes = lax.broadcasted_iota(jnp.int32, (half, half), 1)
    corner = gram[half:, half:]
    cross = gram[half:, :half]
    packed = jnp.where(rows >= lanes, gram[:half, :half], corner)
    diagonal = jnp.sum(jnp.where(rows == lanes, corner, 0.0), axis=0, keepdims=True)
    cross = jnp.pad(cross, ((0, 8), (0, 0)))
    packed = jnp.concatenate([packed, diagonal, jnp.zeros((7, half), jnp.float32)])
    total = jnp.where(mine_first, cross, packed) + swap(jnp.where(mine_first, packed, cross), "col", 1)
    for bit in z_bits:
        total = total + swap(total, "col", bit)
    partner = swap(total, "col", 1)
    orbital_count = piece_rows * row_count * col_count
    return orthonormal(total, partner, filtered, mine_first, row_rank, piece_rows, math.sqrt(orbital_count))


def solution(mesh):
    return jax.shard_map(
        on_device,
        mesh=mesh,
        in_specs=(P("row", "col", None, None), P("row", "col"), P(("col", "row"), None)),
        out_specs=P(("col", "row"), None),
        check_vma=False,
    )
```

```python
import math

import jax
import jax.numpy as jnp
from jax import lax
from jax.experimental import pallas as pl
from jax.experimental.pallas import tpu as pltpu
from jax.sharding import PartitionSpec as P

DEGREE = 4


LOWER = -2.0
CUTOFF = 0.0
UPPER = 2.0


def filter_coefs(degree):
    half_width = (UPPER - CUTOFF) / 2.0
    center = (UPPER + CUTOFF) / 2.0
    sigma_now = half_width / (LOWER - center)
    tau_value = 2.0 / sigma_now
    scales = [sigma_now / half_width]
    carries = [0.0]
    for number in range(1, degree):
        sigma_next = 1.0 / (tau_value - sigma_now)
        scales.append(2.0 * sigma_next / half_width)
        carries.append(sigma_now * sigma_next)
        sigma_now = sigma_next
    return (center, scales, carries)


def swap(value, axis, distance):
    count = lax.axis_size(axis)
    return lax.ppermute(value, axis, [(i, i ^ distance) for i in range(count)])


def bits_below(count):
    return [1 << n for n in range(count.bit_length() - 1)]


def partners(count):
    return [1, *range(count - 1, 1, -1)]


def in_order(values, rank):
    stacked = jnp.stack(list(values.values()))
    distances = jnp.array(list(values), jnp.int32)
    places = jnp.arange(len(values), dtype=jnp.int32)

    def value_of(index):
        place = jnp.sum(jnp.where(distances == (rank ^ index), places, 0))
        return lax.dynamic_index_in_dim(stacked, place, 0, False)

    return jnp.concatenate([value_of(index) for index in range(len(values))])


def densify(blocks, col_index, tile_blocks):
    group_rows, slots, width, _ = blocks.shape
    slots = min(slots, tile_blocks)
    step = max(group_rows // 2, 1)

    def kernel(index_ref, blocks_ref, tile_ref):
        nothing = jnp.zeros((width, width), blocks.dtype)
        for inner in range(step):
            places = [index_ref[pl.program_id(0) * step + inner, slot] for slot in range(slots)]
            places = [jnp.where(place >= 0, lax.rem(place, tile_blocks), -1) for place in places]
            for column in range(tile_blocks):
                value = nothing
                for slot in range(slots):
                    value = jnp.where(places[slot] == column, blocks_ref[inner, slot], value)
                tile_ref[inner * width : (inner + 1) * width, column * width : (column + 1) * width] = value

    return pl.pallas_call(
        kernel,
        grid_spec=pltpu.PrefetchScalarGridSpec(
            num_scalar_prefetch=1,
            grid=(group_rows // step,),
            in_specs=[pl.BlockSpec((step, slots, width, width), lambda i, index: (i, 0, 0, 0))],
            out_specs=pl.BlockSpec((step * width, tile_blocks * width), lambda i, index: (i, 0)),
        ),
        out_shape=jax.ShapeDtypeStruct((group_rows * width, tile_blocks * width), blocks.dtype),
        compiler_params=pltpu.CompilerParams(vmem_limit_bytes=24 << 20),
    )(col_index, blocks)


def exact_dot(a, b, dims):
    return lax.dot_general(
        a, b, (dims, ((), ())), precision=lax.Precision.HIGHEST, preferred_element_type=jnp.float32
    )


def factor(matrix, tall):
    size = matrix.shape[1]
    groups = [matrix[first : first + tall] for first in range(0, size, tall)]
    sub = lax.broadcasted_iota(jnp.int32, (tall, size), 0)
    lane = lax.broadcasted_iota(jnp.int32, (tall, size), 1)
    for number, head in enumerate(groups):
        first = tall * number
        block = (lane >= first) & (lane < first + tall)
        columns = [jnp.broadcast_to(head[:, first + q : first + q + 1], head.shape) for q in range(tall)]
        x = jnp.where(block, jnp.where(lane - first == sub, 1.0, 0.0), head)
        z = x
        pivots = jnp.ones_like(x)
        inverses = jnp.ones_like(x)
        for p in range(tall):
            pivot = columns[p][p : p + 1, :]
            inverse = 1.0 / pivot
            ratio = columns[p] * inverse
            below = jnp.where(sub > p, ratio, 0.0)
            others = jnp.where(sub == p, 0.0, ratio)
            for q in range(p + 1, tall):
                columns[q] = columns[q] - others * columns[q][p : p + 1, :]
            x = x - below * x[p : p + 1, :]
            z = z - others * z[p : p + 1, :]
            pivots = jnp.where(sub == p, pivot, pivots)
            inverses = jnp.where(sub == p, inverse, inverses)
        z = z * inverses
        for later in range(number + 1, len(groups)):
            value = jnp.where(block, 0.0, groups[later])
            for p in range(tall):
                value = value - groups[later][:, first + p : first + p + 1] * z[p : p + 1, :]
            groups[later] = value
        groups[number] = x * lax.rsqrt(pivots)
    return jnp.concatenate(groups)


def orthonormal(total, partner, filtered, mine_first, rank, piece_rows, scale):
    size = total.shape[1]
    tall = 16

    def kernel(flags_ref, total_ref, partner_ref, filtered_ref, out_ref):
        rows = lax.broadcasted_iota(jnp.int32, (size, size), 0)
        lanes = lax.broadcasted_iota(jnp.int32, (size, size), 1)
        is_first = flags_ref[0] != 0
        start = pl.multiple_of(flags_ref[1] * piece_rows, piece_rows)
        cross = jnp.where(is_first, total_ref[:size, :], partner_ref[:size, :])
        both = jnp.where(is_first, partner_ref[:size, :], total_ref[:size, :])
        diagonal = jnp.where(is_first, partner_ref[size : size + 1, :], total_ref[size : size + 1, :])
        mirrored = both.T
        first = factor(jnp.where(rows >= lanes, both, mirrored), tall)
        first = jnp.where(rows >= lanes, first, 0.0)
        below = exact_dot(cross, first, ((1,), (1,)))
        second = jnp.where(lanes > rows, both, mirrored)
        second = jnp.where(lanes == rows, diagonal, second)
        last = factor(second - exact_dot(below, below, ((1,), (1,))), tall)
        last = jnp.where(rows >= lanes, last, 0.0)
        left = exact_dot(filtered_ref[pl.ds(start, piece_rows), :size], first, ((1,), (1,)))
        out_ref[:, :size] = scale * left
        right = filtered_ref[pl.ds(start, piece_rows), size:] - exact_dot(left, below, ((1,), (1,)))
        out_ref[:, size:] = scale * exact_dot(right, last, ((1,), (1,)))

    vmem = pl.BlockSpec(memory_space=pltpu.VMEM)
    return pl.pallas_call(
        kernel,
        in_specs=[pl.BlockSpec(memory_space=pltpu.SMEM), vmem, vmem, vmem],
        out_specs=vmem,
        out_shape=jax.ShapeDtypeStruct((piece_rows, 2 * size), jnp.float32),
        compiler_params=pltpu.CompilerParams(vmem_limit_bytes=8 << 20),
    )(jnp.stack([mine_first.astype(jnp.int32), rank]), total, partner, filtered)


def on_device(blocks, col_index, vectors):
    center, scales, carries = filter_coefs(DEGREE)
    row_count = lax.axis_size("row")
    col_count = lax.axis_size("col")
    row_rank = lax.axis_index("row")
    col_rank = lax.axis_index("col")
    core = col_rank % 2
    group_rows, _, width, _ = blocks.shape
    piece_rows, states = vectors.shape
    half = states // 2
    tile_blocks = piece_rows // width * row_count
    tile_rows = tile_blocks * width
    row_bits = bits_below(row_count)
    z_count = col_count // 2
    z_rank = col_rank // 2
    narrow = jnp.bfloat16

    mine_first = core == 0

    def kept_and_sent(value):
        left, right = value[:, :half], value[:, half:]
        return jnp.where(mine_first, left, right), jnp.where(mine_first, right, left)

    low_start = vectors.astype(narrow)
    arrived = {0: low_start, **{k: swap(low_start, "row", k) for k in partners(row_count)}}
    low_own, sent = kept_and_sent(in_order(arrived, row_rank))
    low_other = swap(sent, "col", 1)
    own_start, sent = kept_and_sent(vectors)
    other_start = swap(sent, "col", 1)

    own = densify(blocks, col_index, tile_blocks)
    other = swap(own, "col", 1)

    first_row = row_rank * group_rows
    own_offset = first_row - col_rank * tile_blocks
    other_offset = first_row - (col_rank ^ 1) * tile_blocks

    segments = group_rows // tile_blocks

    def spread(low, offset):
        value = low.astype(jnp.float32)
        return jnp.concatenate(
            [jnp.where(offset == -k * tile_blocks, value, 0.0) for k in range(segments)]
        )

    def picked(low, offset):
        value = low.astype(jnp.float32).reshape(segments, tile_rows, half)
        parts = [jnp.where(offset == -k * tile_blocks, value[k], 0.0) for k in range(segments)]
        return sum(parts[1:], parts[0])

    def forward(low_own, low_other):
        product = jnp.dot(own, low_own, preferred_element_type=jnp.float32)
        product = product + jnp.dot(other, low_other, preferred_element_type=jnp.float32)
        return product - center * (spread(low_own, own_offset) + spread(low_other, other_offset))

    def backward(low):
        def part(tile, offset):
            product = lax.dot_general(tile, low, (((0,), (0,)), ((), ())), preferred_element_type=jnp.float32)
            return product - center * picked(low, offset)

        return part(own, own_offset), part(other, other_offset)

    def piece_of(value, index):
        rows = value.shape[0] // z_count
        return lax.dynamic_slice_in_dim(value, index * rows, rows, 0)

    def sum_over_z(value):
        sent = value.astype(narrow)
        total = piece_of(value, z_rank)
        for k in partners(z_count):
            total = total + swap(piece_of(sent, z_rank ^ k), "col", 2 * k).astype(jnp.float32)
        return total

    def gather_over_z(value):
        return in_order({0: value, **{k: swap(value, "col", 2 * k) for k in partners(z_count)}}, z_rank)

    def sum_over_row(one, two):
        for level, (bit_one, bit_two) in enumerate(zip(row_bits, reversed(row_bits))):
            sent = narrow if level < 2 else jnp.float32
            low_one, low_two = lax.optimization_barrier((one.astype(sent), two.astype(sent)))
            from_one, from_two = lax.optimization_barrier(
                (swap(low_one, "row", bit_one), swap(low_two, "row", bit_two))
            )
            one = low_one.astype(jnp.float32) + from_one.astype(jnp.float32)
            two = low_two.astype(jnp.float32) + from_two.astype(jnp.float32)
        return one, two

    def placed(piece):
        here = jnp.arange(row_count)[:, None, None] == row_rank
        return jnp.where(here, piece[None], 0.0).reshape(tile_rows, half)

    y1 = scales[0] * sum_over_z(forward(low_own, low_other))
    low = gather_over_z(y1.astype(narrow))
    part_own, part_other = backward(low)
    y2_own, y2_other = sum_over_row(
        scales[1] * part_own - carries[1] * placed(own_start),
        scales[1] * part_other - carries[1] * placed(other_start),
    )
    y3 = scales[2] * sum_over_z(forward(y2_own.astype(narrow), y2_other.astype(narrow))) - carries[2] * y1
    low = gather_over_z(y3.astype(narrow))
    part_own, part_other = backward(low)
    image_own, image_other = sum_over_row(part_own, part_other)
    y4_own = scales[3] * image_own - carries[3] * y2_own
    y4_other = scales[3] * image_other - carries[3] * y2_other

    partner = swap(y4_other, "col", 1)
    filtered = jnp.concatenate(
        [jnp.where(mine_first, y4_own, partner), jnp.where(mine_first, partner, y4_own)], axis=1
    )
    gram = exact_dot(filtered, filtered, ((0,), (0,)))
    rows = lax.broadcasted_iota(jnp.int32, (half, half), 0)
    lanes = lax.broadcasted_iota(jnp.int32, (half, half), 1)
    corner = gram[half:, half:]
    cross = gram[half:, :half]
    packed = jnp.where(rows >= lanes, gram[:half, :half], corner)
    diagonal = jnp.sum(jnp.where(rows == lanes, corner, 0.0), axis=0, keepdims=True)
    cross = jnp.pad(cross, ((0, 8), (0, 0)))
    packed = jnp.concatenate([packed, diagonal, jnp.zeros((7, half), jnp.float32)])
    total = jnp.where(mine_first, cross, packed) + swap(jnp.where(mine_first, packed, cross), "col", 1)
    total = sum([swap(total, "col", 2 * k) for k in partners(z_count)], total)
    partner = swap(total, "col", 1)
    orbital_count = piece_rows * row_count * col_count
    return orthonormal(total, partner, filtered, mine_first, row_rank, piece_rows, math.sqrt(orbital_count))


def solution(mesh):
    return jax.shard_map(
        on_device,
        mesh=mesh,
        in_specs=(P("row", "col", None, None), P("row", "col"), P(("col", "row"), None)),
        out_specs=P(("col", "row"), None),
        check_vma=False,
    )
```

```python
import math

import jax
import jax.numpy as jnp
from jax import lax
from jax.experimental import pallas as pl
from jax.experimental.pallas import tpu as pltpu
from jax.sharding import PartitionSpec as P

DEGREE = 4


LOWER = -2.0
CUTOFF = 0.0
UPPER = 2.0


def filter_coefs(degree):
    half_width = (UPPER - CUTOFF) / 2.0
    center = (UPPER + CUTOFF) / 2.0
    sigma_now = half_width / (LOWER - center)
    tau_value = 2.0 / sigma_now
    scales = [sigma_now / half_width]
    carries = [0.0]
    for number in range(1, degree):
        sigma_next = 1.0 / (tau_value - sigma_now)
        scales.append(2.0 * sigma_next / half_width)
        carries.append(sigma_now * sigma_next)
        sigma_now = sigma_next
    return (center, scales, carries)


def swap(value, axis, distance):
    count = lax.axis_size(axis)
    return lax.ppermute(value, axis, [(i, i ^ distance) for i in range(count)])


def bits_below(count):
    return [1 << n for n in range(count.bit_length() - 1)]


def partners(count):
    return [1, *range(count - 1, 1, -1)]


def in_order(values, rank):
    stacked = jnp.stack(list(values.values()))

    def value_of(index):
        place = rank ^ index
        for number, distance in enumerate(values):
            if number != distance:
                place = jnp.where((rank ^ index) == distance, number, place)
        return lax.dynamic_index_in_dim(stacked, place, 0, False)

    return jnp.concatenate([value_of(index) for index in range(len(values))])


def densify(blocks, col_index, tile_blocks):
    group_rows, slots, width, _ = blocks.shape
    slots = min(slots, tile_blocks)
    step = max(group_rows // 2, 1)

    def kernel(index_ref, blocks_ref, tile_ref):
        nothing = jnp.zeros((width, width), blocks.dtype)
        for inner in range(step):
            places = [index_ref[pl.program_id(0) * step + inner, slot] for slot in range(slots)]
            places = [jnp.where(place >= 0, lax.rem(place, tile_blocks), -1) for place in places]
            for column in range(tile_blocks):
                value = nothing
                for slot in range(slots):
                    value = jnp.where(places[slot] == column, blocks_ref[inner, slot], value)
                tile_ref[inner * width : (inner + 1) * width, column * width : (column + 1) * width] = value

    return pl.pallas_call(
        kernel,
        grid_spec=pltpu.PrefetchScalarGridSpec(
            num_scalar_prefetch=1,
            grid=(group_rows // step,),
            in_specs=[pl.BlockSpec((step, slots, width, width), lambda i, index: (i, 0, 0, 0))],
            out_specs=pl.BlockSpec((step * width, tile_blocks * width), lambda i, index: (i, 0)),
        ),
        out_shape=jax.ShapeDtypeStruct((group_rows * width, tile_blocks * width), blocks.dtype),
        compiler_params=pltpu.CompilerParams(vmem_limit_bytes=24 << 20),
    )(col_index, blocks)


def exact_dot(a, b, dims):
    return lax.dot_general(
        a, b, (dims, ((), ())), precision=lax.Precision.HIGHEST, preferred_element_type=jnp.float32
    )


def factor(matrix, tall):
    size = matrix.shape[1]
    groups = [matrix[first : first + tall] for first in range(0, size, tall)]
    sub = lax.broadcasted_iota(jnp.int32, (tall, size), 0)
    lane = lax.broadcasted_iota(jnp.int32, (tall, size), 1)
    for number, head in enumerate(groups):
        first = tall * number
        block = (lane >= first) & (lane < first + tall)
        columns = [jnp.broadcast_to(head[:, first + q : first + q + 1], head.shape) for q in range(tall)]
        x = jnp.where(block, jnp.where(lane - first == sub, 1.0, 0.0), head)
        z = x
        pivots = jnp.ones_like(x)
        inverses = jnp.ones_like(x)
        for p in range(tall):
            pivot = columns[p][p : p + 1, :]
            inverse = 1.0 / pivot
            ratio = columns[p] * inverse
            below = jnp.where(sub > p, ratio, 0.0)
            others = jnp.where(sub == p, 0.0, ratio)
            for q in range(p + 1, tall):
                columns[q] = columns[q] - others * columns[q][p : p + 1, :]
            x = x - below * x[p : p + 1, :]
            z = z - others * z[p : p + 1, :]
            pivots = jnp.where(sub == p, pivot, pivots)
            inverses = jnp.where(sub == p, inverse, inverses)
        z = z * inverses
        for later in range(number + 1, len(groups)):
            value = jnp.where(block, 0.0, groups[later])
            for p in range(tall):
                value = value - groups[later][:, first + p : first + p + 1] * z[p : p + 1, :]
            groups[later] = value
        groups[number] = x * lax.rsqrt(pivots)
    return jnp.concatenate(groups)


def orthonormal(total, partner, filtered, mine_first, rank, piece_rows, scale):
    size = total.shape[1]
    tall = 16

    def kernel(flags_ref, total_ref, partner_ref, filtered_ref, out_ref):
        rows = lax.broadcasted_iota(jnp.int32, (size, size), 0)
        lanes = lax.broadcasted_iota(jnp.int32, (size, size), 1)
        is_first = flags_ref[0] != 0
        start = pl.multiple_of(flags_ref[1] * piece_rows, piece_rows)
        cross = jnp.where(is_first, total_ref[:size, :], partner_ref[:size, :])
        both = jnp.where(is_first, partner_ref[:size, :], total_ref[:size, :])
        diagonal = jnp.where(is_first, partner_ref[size : size + 1, :], total_ref[size : size + 1, :])
        mirrored = both.T
        first = factor(jnp.where(rows >= lanes, both, mirrored), tall)
        first = jnp.where(rows >= lanes, first, 0.0)
        below = exact_dot(cross, first, ((1,), (1,)))
        second = jnp.where(lanes > rows, both, mirrored)
        second = jnp.where(lanes == rows, diagonal, second)
        last = factor(second - exact_dot(below, below, ((1,), (1,))), tall)
        last = jnp.where(rows >= lanes, last, 0.0)
        left = exact_dot(filtered_ref[pl.ds(start, piece_rows), :size], first, ((1,), (1,)))
        out_ref[:, :size] = scale * left
        right = filtered_ref[pl.ds(start, piece_rows), size:] - exact_dot(left, below, ((1,), (1,)))
        out_ref[:, size:] = scale * exact_dot(right, last, ((1,), (1,)))

    vmem = pl.BlockSpec(memory_space=pltpu.VMEM)
    return pl.pallas_call(
        kernel,
        in_specs=[pl.BlockSpec(memory_space=pltpu.SMEM), vmem, vmem, vmem],
        out_specs=vmem,
        out_shape=jax.ShapeDtypeStruct((piece_rows, 2 * size), jnp.float32),
        compiler_params=pltpu.CompilerParams(vmem_limit_bytes=8 << 20),
    )(jnp.stack([mine_first.astype(jnp.int32), rank]), total, partner, filtered)


def on_device(blocks, col_index, vectors):
    center, scales, carries = filter_coefs(DEGREE)
    row_count = lax.axis_size("row")
    col_count = lax.axis_size("col")
    row_rank = lax.axis_index("row")
    col_rank = lax.axis_index("col")
    core = col_rank % 2
    group_rows, _, width, _ = blocks.shape
    piece_rows, states = vectors.shape
    half = states // 2
    tile_blocks = piece_rows // width * row_count
    tile_rows = tile_blocks * width
    row_bits = bits_below(row_count)
    z_count = col_count // 2
    z_rank = col_rank // 2
    narrow = jnp.bfloat16

    mine_first = core == 0

    def kept_and_sent(value):
        left, right = value[:, :half], value[:, half:]
        return jnp.where(mine_first, left, right), jnp.where(mine_first, right, left)

    low_start = vectors.astype(narrow)
    arrived = {0: low_start, **{k: swap(low_start, "row", k) for k in partners(row_count)}}
    low_own, sent = kept_and_sent(in_order(arrived, row_rank))
    low_other = swap(sent, "col", 1)
    own_start, sent = kept_and_sent(vectors)
    other_start = swap(sent, "col", 1)

    own = densify(blocks, col_index, tile_blocks)
    other = swap(own, "col", 1)

    first_row = row_rank * group_rows
    own_offset = first_row - col_rank * tile_blocks
    other_offset = first_row - (col_rank ^ 1) * tile_blocks

    segments = group_rows // tile_blocks

    def spread(low, offset):
        value = low.astype(jnp.float32)
        return jnp.concatenate(
            [jnp.where(offset == -k * tile_blocks, value, 0.0) for k in range(segments)]
        )

    def picked(low, offset):
        value = low.astype(jnp.float32).reshape(segments, tile_rows, half)
        parts = [jnp.where(offset == -k * tile_blocks, value[k], 0.0) for k in range(segments)]
        return sum(parts[1:], parts[0])

    def forward(low_own, low_other):
        product = jnp.dot(own, low_own, preferred_element_type=jnp.float32)
        product = product + jnp.dot(other, low_other, preferred_element_type=jnp.float32)
        return product - center * (spread(low_own, own_offset) + spread(low_other, other_offset))

    def backward(low):
        def part(tile, offset):
            product = lax.dot_general(tile, low, (((0,), (0,)), ((), ())), preferred_element_type=jnp.float32)
            return product - center * picked(low, offset)

        return part(own, own_offset), part(other, other_offset)

    def piece_of(value, index):
        rows = value.shape[0] // z_count
        return lax.dynamic_slice_in_dim(value, index * rows, rows, 0)

    def sum_over_z(value):
        sent = value.astype(narrow)
        total = piece_of(value, z_rank)
        for k in partners(z_count):
            total = total + swap(piece_of(sent, z_rank ^ k), "col", 2 * k).astype(jnp.float32)
        return total

    def gather_over_z(value):
        return in_order({0: value, **{k: swap(value, "col", 2 * k) for k in partners(z_count)}}, z_rank)

    def sum_over_row(one, two):
        for level, (bit_one, bit_two) in enumerate(zip(row_bits, reversed(row_bits))):
            sent = narrow if level < 2 else jnp.float32
            low_one, low_two = lax.optimization_barrier((one.astype(sent), two.astype(sent)))
            from_one, from_two = lax.optimization_barrier(
                (swap(low_one, "row", bit_one), swap(low_two, "row", bit_two))
            )
            one = low_one.astype(jnp.float32) + from_one.astype(jnp.float32)
            two = low_two.astype(jnp.float32) + from_two.astype(jnp.float32)
        return one, two

    def placed(piece):
        here = jnp.arange(row_count)[:, None, None] == row_rank
        return jnp.where(here, piece[None], 0.0).reshape(tile_rows, half)

    y1 = scales[0] * sum_over_z(forward(low_own, low_other))
    low = gather_over_z(y1.astype(narrow))
    part_own, part_other = backward(low)
    y2_own, y2_other = sum_over_row(
        scales[1] * part_own - carries[1] * placed(own_start),
        scales[1] * part_other - carries[1] * placed(other_start),
    )
    y3 = scales[2] * sum_over_z(forward(y2_own.astype(narrow), y2_other.astype(narrow))) - carries[2] * y1
    low = gather_over_z(y3.astype(narrow))
    part_own, part_other = backward(low)
    image_own, image_other = sum_over_row(part_own, part_other)
    y4_own = scales[3] * image_own - carries[3] * y2_own
    y4_other = scales[3] * image_other - carries[3] * y2_other

    partner = swap(y4_other, "col", 1)
    filtered = jnp.concatenate(
        [jnp.where(mine_first, y4_own, partner), jnp.where(mine_first, partner, y4_own)], axis=1
    )
    gram = exact_dot(filtered, filtered, ((0,), (0,)))
    rows = lax.broadcasted_iota(jnp.int32, (half, half), 0)
    lanes = lax.broadcasted_iota(jnp.int32, (half, half), 1)
    corner = gram[half:, half:]
    cross = gram[half:, :half]
    packed = jnp.where(rows >= lanes, gram[:half, :half], corner)
    diagonal = jnp.sum(jnp.where(rows == lanes, corner, 0.0), axis=0, keepdims=True)
    cross = jnp.pad(cross, ((0, 8), (0, 0)))
    packed = jnp.concatenate([packed, diagonal, jnp.zeros((7, half), jnp.float32)])
    total = jnp.where(mine_first, cross, packed) + swap(jnp.where(mine_first, packed, cross), "col", 1)
    total = sum([swap(total, "col", 2 * k) for k in partners(z_count)], total)
    partner = swap(total, "col", 1)
    orbital_count = piece_rows * row_count * col_count
    return orthonormal(total, partner, filtered, mine_first, row_rank, piece_rows, math.sqrt(orbital_count))


def solution(mesh):
    return jax.shard_map(
        on_device,
        mesh=mesh,
        in_specs=(P("row", "col", None, None), P("row", "col"), P(("col", "row"), None)),
        out_specs=P(("col", "row"), None),
        check_vma=False,
    )
```

```python
import math

import jax
import jax.numpy as jnp
from jax import lax
from jax.experimental import pallas as pl
from jax.experimental.pallas import tpu as pltpu
from jax.sharding import PartitionSpec as P

DEGREE = 4


LOWER = -2.0
CUTOFF = 0.0
UPPER = 2.0


def filter_coefs(degree):
    half_width = (UPPER - CUTOFF) / 2.0
    center = (UPPER + CUTOFF) / 2.0
    sigma_now = half_width / (LOWER - center)
    tau_value = 2.0 / sigma_now
    scales = [sigma_now / half_width]
    carries = [0.0]
    for number in range(1, degree):
        sigma_next = 1.0 / (tau_value - sigma_now)
        scales.append(2.0 * sigma_next / half_width)
        carries.append(sigma_now * sigma_next)
        sigma_now = sigma_next
    return (center, scales, carries)


def swap(value, axis, distance):
    count = lax.axis_size(axis)
    return lax.ppermute(value, axis, [(i, i ^ distance) for i in range(count)])


def bits_below(count):
    return [1 << n for n in range(count.bit_length() - 1)]


def partners(count):
    return [1, *range(count - 1, 1, -1)]


def in_order(values, rank):
    stacked = jnp.stack(list(values.values()))

    def value_of(index):
        place = rank ^ index
        for number, distance in enumerate(values):
            if number != distance:
                place = jnp.where((rank ^ index) == distance, number, place)
        return lax.dynamic_index_in_dim(stacked, place, 0, False)

    return jnp.concatenate([value_of(index) for index in range(len(values))])


def densify(blocks, col_index, tile_blocks):
    group_rows, slots, width, _ = blocks.shape
    slots = min(slots, tile_blocks)
    step = max(group_rows // 2, 1)

    def kernel(index_ref, blocks_ref, tile_ref):
        nothing = jnp.zeros((width, width), blocks.dtype)
        for inner in range(step):
            places = [index_ref[pl.program_id(0) * step + inner, slot] for slot in range(slots)]
            places = [jnp.where(place >= 0, lax.rem(place, tile_blocks), -1) for place in places]
            for column in range(tile_blocks):
                value = nothing
                for slot in range(slots):
                    value = jnp.where(places[slot] == column, blocks_ref[inner, slot], value)
                tile_ref[inner * width : (inner + 1) * width, column * width : (column + 1) * width] = value

    return pl.pallas_call(
        kernel,
        grid_spec=pltpu.PrefetchScalarGridSpec(
            num_scalar_prefetch=1,
            grid=(group_rows // step,),
            in_specs=[pl.BlockSpec((step, slots, width, width), lambda i, index: (i, 0, 0, 0))],
            out_specs=pl.BlockSpec((step * width, tile_blocks * width), lambda i, index: (i, 0)),
        ),
        out_shape=jax.ShapeDtypeStruct((group_rows * width, tile_blocks * width), blocks.dtype),
        compiler_params=pltpu.CompilerParams(vmem_limit_bytes=24 << 20),
    )(col_index, blocks)


def exact_dot(a, b, dims):
    return lax.dot_general(
        a, b, (dims, ((), ())), precision=lax.Precision.HIGHEST, preferred_element_type=jnp.float32
    )


def tree_sum(terms):
    while len(terms) > 1:
        terms = [sum(terms[n + 1 : n + 2], terms[n]) for n in range(0, len(terms), 2)]
    return terms[0]


def factor(matrix, tall):
    size = matrix.shape[1]
    groups = [matrix[first : first + tall] for first in range(0, size, tall)]
    sub = lax.broadcasted_iota(jnp.int32, (tall, size), 0)
    lane = lax.broadcasted_iota(jnp.int32, (tall, size), 1)
    for number, head in enumerate(groups):
        first = tall * number
        block = (lane >= first) & (lane < first + tall)
        columns = [jnp.broadcast_to(head[:, first + q : first + q + 1], head.shape) for q in range(tall)]
        x = jnp.where(block, jnp.where(lane - first == sub, 1.0, 0.0), head)
        z = x
        pivots = jnp.ones_like(x)
        inverses = jnp.ones_like(x)
        for p in range(tall):
            pivot = columns[p][p : p + 1, :]
            inverse = 1.0 / pivot
            masked = jnp.where(sub == p, 0.0, columns[p])
            others = masked * inverse
            below = jnp.where(sub > p, others, 0.0)
            for q in range(p + 1, tall):
                if q == p + 1:
                    columns[q] = columns[q] - (masked * columns[q][p : p + 1, :]) * inverse
                else:
                    columns[q] = columns[q] - others * columns[q][p : p + 1, :]
            x = x - below * x[p : p + 1, :]
            z = z - others * z[p : p + 1, :]
            pivots = jnp.where(sub == p, pivot, pivots)
            inverses = jnp.where(sub == p, inverse, inverses)
        z = z * inverses
        if number + 1 < len(groups):
            following = groups[number + 1]
            terms = [following[:, first + p : first + p + 1] * z[p : p + 1, :] for p in range(tall)]
            groups[number + 1] = jnp.where(block, 0.0, following) - tree_sum(terms)
        if number + 2 < len(groups):
            rest = jnp.concatenate(groups[number + 2 :])
            lanes = lax.broadcasted_iota(jnp.int32, rest.shape, 1)
            gone = (lanes >= first) & (lanes < first + tall)
            placed = [jnp.zeros((first, size), jnp.float32)] if first else []
            placed = jnp.concatenate([*placed, z, jnp.zeros((size - first - tall, size), jnp.float32)])
            rest = jnp.where(gone, 0.0, rest) - exact_dot(rest, placed, ((1,), (0,)))
            groups[number + 2 :] = [rest[n : n + tall] for n in range(0, rest.shape[0], tall)]
        groups[number] = x * lax.rsqrt(pivots)
    return jnp.concatenate(groups)


def orthonormal(total, partner, mine, theirs, mine_first, scale):
    size = total.shape[1]
    tall = 16

    def kernel(first_ref, total_ref, partner_ref, mine_ref, theirs_ref, out_ref):
        rows = lax.broadcasted_iota(jnp.int32, (size, size), 0)
        lanes = lax.broadcasted_iota(jnp.int32, (size, size), 1)
        is_first = first_ref[0] != 0
        cross = jnp.where(is_first, total_ref[:size, :], partner_ref[:size, :])
        both = jnp.where(is_first, partner_ref[:size, :], total_ref[:size, :])
        diagonal = jnp.where(is_first, partner_ref[size : size + 1, :], total_ref[size : size + 1, :])
        mirrored = both.T
        first = factor(jnp.where(rows >= lanes, both, mirrored), tall)
        first = jnp.where(rows >= lanes, first, 0.0)
        below = exact_dot(cross, first, ((1,), (1,)))
        second = jnp.where(lanes > rows, both, mirrored)
        second = jnp.where(lanes == rows, diagonal, second)
        last = factor(second - exact_dot(below, below, ((1,), (1,))), tall)
        last = jnp.where(rows >= lanes, last, 0.0)
        left = jnp.where(is_first, mine_ref[...], theirs_ref[...])
        left = exact_dot(left, first, ((1,), (1,)))
        out_ref[:, :size] = scale * left
        right = jnp.where(is_first, theirs_ref[...], mine_ref[...]) - exact_dot(left, below, ((1,), (1,)))
        out_ref[:, size:] = scale * exact_dot(right, last, ((1,), (1,)))

    vmem = pl.BlockSpec(memory_space=pltpu.VMEM)
    return pl.pallas_call(
        kernel,
        in_specs=[pl.BlockSpec(memory_space=pltpu.SMEM), vmem, vmem, vmem, vmem],
        out_specs=vmem,
        out_shape=jax.ShapeDtypeStruct((mine.shape[0], 2 * size), jnp.float32),
        compiler_params=pltpu.CompilerParams(vmem_limit_bytes=8 << 20),
    )(mine_first.astype(jnp.int32).reshape(1), total, partner, mine, theirs)


def on_device(blocks, col_index, vectors):
    center, scales, carries = filter_coefs(DEGREE)
    row_count = lax.axis_size("row")
    col_count = lax.axis_size("col")
    row_rank = lax.axis_index("row")
    col_rank = lax.axis_index("col")
    core = col_rank % 2
    group_rows, _, width, _ = blocks.shape
    piece_rows, states = vectors.shape
    half = states // 2
    tile_blocks = piece_rows // width * row_count
    tile_rows = tile_blocks * width
    row_bits = bits_below(row_count)
    z_count = col_count // 2
    z_bits = [2 * bit for bit in bits_below(z_count)]
    narrow = jnp.bfloat16

    mine_first = core == 0

    def kept_and_sent(value):
        left, right = value[:, :half], value[:, half:]
        return jnp.where(mine_first, left, right), jnp.where(mine_first, right, left)

    low_start = vectors.astype(narrow)
    arrived = {0: low_start, **{k: swap(low_start, "row", k) for k in partners(row_count)}}
    low_own, sent = kept_and_sent(in_order(arrived, row_rank))
    low_other = swap(sent, "col", 1)
    own_start, sent = kept_and_sent(vectors)
    other_start = swap(sent, "col", 1)

    own = densify(blocks, col_index, tile_blocks)
    other = swap(own, "col", 1)

    first_row = row_rank * group_rows
    own_offset = first_row - col_rank * tile_blocks
    other_offset = first_row - (col_rank ^ 1) * tile_blocks

    segments = group_rows // tile_blocks

    def spread(low, offset):
        value = low.astype(jnp.float32)
        return jnp.concatenate(
            [jnp.where(offset == -k * tile_blocks, value, 0.0) for k in range(segments)]
        )

    def picked(low, offset):
        value = low.astype(jnp.float32).reshape(segments, tile_rows, half)
        parts = [jnp.where(offset == -k * tile_blocks, value[k], 0.0) for k in range(segments)]
        return sum(parts[1:], parts[0])

    def forward(low_own, low_other):
        product = jnp.dot(own, low_own, preferred_element_type=jnp.float32)
        product = product + jnp.dot(other, low_other, preferred_element_type=jnp.float32)
        product = product - center * (spread(low_own, own_offset) + spread(low_other, other_offset))
        middle = product.shape[0] // 2
        return product[:middle], product[middle:]

    def backward(low):
        def part(tile, offset):
            product = lax.dot_general(tile, low, (((0,), (0,)), ((), ())), preferred_element_type=jnp.float32)
            return product - center * picked(low, offset)

        return part(own, own_offset), part(other, other_offset)

    def sum_over(axis, bits, one, two):
        for bit_one, bit_two in zip(bits, reversed(bits)):
            from_one, from_two = lax.optimization_barrier(
                (swap(one.astype(narrow), axis, bit_one), swap(two.astype(narrow), axis, bit_two))
            )
            one, two = one + from_one.astype(jnp.float32), two + from_two.astype(jnp.float32)
        return one, two

    def placed(piece):
        here = jnp.arange(row_count)[:, None, None] == row_rank
        return jnp.where(here, piece[None], 0.0).reshape(tile_rows, half)

    y1_one, y1_two = [
        scales[0] * image for image in sum_over("col", z_bits, *forward(low_own, low_other))
    ]
    part_own, part_other = backward(jnp.concatenate([y1_one.astype(narrow), y1_two.astype(narrow)]))
    y2_own, y2_other = sum_over(
        "row",
        row_bits,
        scales[1] * part_own - carries[1] * placed(own_start),
        scales[1] * part_other - carries[1] * placed(other_start),
    )
    image_one, image_two = sum_over(
        "col", z_bits, *forward(y2_own.astype(narrow), y2_other.astype(narrow))
    )
    low_one = (scales[2] * image_one - carries[2] * y1_one).astype(narrow)
    low_two = (scales[2] * image_two - carries[2] * y1_two).astype(narrow)
    part_own, part_other = backward(jnp.concatenate([low_one, low_two]))
    image_own, image_other = sum_over("row", row_bits, part_own, part_other)
    y4_own = scales[3] * image_own - carries[3] * y2_own
    y4_other = scales[3] * image_other - carries[3] * y2_other

    mine = jnp.concatenate([y4_own, y4_other])
    theirs = swap(jnp.concatenate([y4_other, y4_own]), "col", 1)
    corner = exact_dot(mine, mine, ((0,), (0,)))
    cross = exact_dot(theirs, jnp.where(mine_first, mine, theirs), ((0,), (0,)))
    rows = lax.broadcasted_iota(jnp.int32, (half, half), 0)
    lanes = lax.broadcasted_iota(jnp.int32, (half, half), 1)
    packed = jnp.where(mine_first | (rows >= lanes), cross, corner)
    diagonal = jnp.sum(jnp.where(rows == lanes, corner, 0.0), axis=0, keepdims=True)
    total = jnp.concatenate([packed, jnp.pad(diagonal, ((0, 7), (0, 0)))])
    total = sum([swap(total, "col", 2 * k) for k in partners(z_count)], total)
    partner = swap(total, "col", 1)
    orbital_count = piece_rows * row_count * col_count
    here = row_rank * piece_rows
    mine = lax.dynamic_slice_in_dim(mine, here, piece_rows, 0)
    theirs = lax.dynamic_slice_in_dim(theirs, here, piece_rows, 0)
    return orthonormal(total, partner, mine, theirs, mine_first, math.sqrt(orbital_count))


def solution(mesh):
    return jax.shard_map(
        on_device,
        mesh=mesh,
        in_specs=(P("row", "col", None, None), P("row", "col"), P(("col", "row"), None)),
        out_specs=P(("col", "row"), None),
        check_vma=False,
    )
```

```python
import math

import jax
import jax.numpy as jnp
from jax import lax
from jax.experimental import pallas as pl
from jax.experimental.pallas import tpu as pltpu
from jax.sharding import PartitionSpec as P

DEGREE = 4


LOWER = -2.0
CUTOFF = 0.0
UPPER = 2.0


def filter_coefs(degree):
    half_width = (UPPER - CUTOFF) / 2.0
    center = (UPPER + CUTOFF) / 2.0
    sigma_now = half_width / (LOWER - center)
    tau_value = 2.0 / sigma_now
    scales = [sigma_now / half_width]
    carries = [0.0]
    for number in range(1, degree):
        sigma_next = 1.0 / (tau_value - sigma_now)
        scales.append(2.0 * sigma_next / half_width)
        carries.append(sigma_now * sigma_next)
        sigma_now = sigma_next
    return (center, scales, carries)


def swap(value, axis, distance):
    count = lax.axis_size(axis)
    return lax.ppermute(value, axis, [(i, i ^ distance) for i in range(count)])


def bits_below(count):
    return [1 << n for n in range(count.bit_length() - 1)]


def partners(count):
    return [1, *range(count - 1, 1, -1)]


def in_order(values, rank):
    stacked = jnp.stack(list(values.values()))

    def value_of(index):
        place = rank ^ index
        for number, distance in enumerate(values):
            if number != distance:
                place = jnp.where((rank ^ index) == distance, number, place)
        return lax.dynamic_index_in_dim(stacked, place, 0, False)

    return jnp.concatenate([value_of(index) for index in range(len(values))])


def densify(blocks, col_index, tile_blocks):
    group_rows, slots, width, _ = blocks.shape
    slots = min(slots, tile_blocks)
    step = max(group_rows // 2, 1)

    def kernel(index_ref, blocks_ref, tile_ref):
        nothing = jnp.zeros((width, width), blocks.dtype)
        for inner in range(step):
            places = [index_ref[pl.program_id(0) * step + inner, slot] for slot in range(slots)]
            places = [jnp.where(place >= 0, lax.rem(place, tile_blocks), -1) for place in places]
            for column in range(tile_blocks):
                value = nothing
                for slot in range(slots):
                    value = jnp.where(places[slot] == column, blocks_ref[inner, slot], value)
                tile_ref[inner * width : (inner + 1) * width, column * width : (column + 1) * width] = value

    return pl.pallas_call(
        kernel,
        grid_spec=pltpu.PrefetchScalarGridSpec(
            num_scalar_prefetch=1,
            grid=(group_rows // step,),
            in_specs=[pl.BlockSpec((step, slots, width, width), lambda i, index: (i, 0, 0, 0))],
            out_specs=pl.BlockSpec((step * width, tile_blocks * width), lambda i, index: (i, 0)),
        ),
        out_shape=jax.ShapeDtypeStruct((group_rows * width, tile_blocks * width), blocks.dtype),
        compiler_params=pltpu.CompilerParams(vmem_limit_bytes=24 << 20),
    )(col_index, blocks)


def exact_dot(a, b, dims):
    return lax.dot_general(
        a, b, (dims, ((), ())), precision=lax.Precision.HIGHEST, preferred_element_type=jnp.float32
    )


def tree_sum(terms):
    while len(terms) > 1:
        terms = [sum(terms[n + 1 : n + 2], terms[n]) for n in range(0, len(terms), 2)]
    return terms[0]


def factor(matrix, tall):
    size = matrix.shape[1]
    groups = [matrix[first : first + tall] for first in range(0, size, tall)]
    sub = lax.broadcasted_iota(jnp.int32, (tall, size), 0)
    lane = lax.broadcasted_iota(jnp.int32, (tall, size), 1)
    for number, head in enumerate(groups):
        first = tall * number
        block = (lane >= first) & (lane < first + tall)
        columns = [jnp.broadcast_to(head[:, first + q : first + q + 1], head.shape) for q in range(tall)]
        x = jnp.where(block, jnp.where(lane - first == sub, 1.0, 0.0), head)
        z = x
        pivots = jnp.ones_like(x)
        inverses = jnp.ones_like(x)
        for p in range(tall):
            pivot = columns[p][p : p + 1, :]
            inverse = 1.0 / pivot
            masked = jnp.where(sub == p, 0.0, columns[p])
            others = masked * inverse
            below = jnp.where(sub > p, others, 0.0)
            for q in range(p + 1, tall):
                if q == p + 1:
                    columns[q] = columns[q] - (masked * columns[q][p : p + 1, :]) * inverse
                else:
                    columns[q] = columns[q] - others * columns[q][p : p + 1, :]
            x = x - below * x[p : p + 1, :]
            z = z - others * z[p : p + 1, :]
            pivots = jnp.where(sub == p, pivot, pivots)
            inverses = jnp.where(sub == p, inverse, inverses)
        z = z * inverses
        if number + 1 < len(groups):
            following = groups[number + 1]
            terms = [following[:, first + p : first + p + 1] * z[p : p + 1, :] for p in range(tall)]
            groups[number + 1] = jnp.where(block, 0.0, following) - tree_sum(terms)
        if number + 2 < len(groups):
            rest = jnp.concatenate(groups[number + 2 :])
            lanes = lax.broadcasted_iota(jnp.int32, rest.shape, 1)
            gone = (lanes >= first) & (lanes < first + tall)
            placed = [jnp.zeros((first, size), jnp.float32)] if first else []
            placed = jnp.concatenate([*placed, z, jnp.zeros((size - first - tall, size), jnp.float32)])
            rest = jnp.where(gone, 0.0, rest) - exact_dot(rest, placed, ((1,), (0,)))
            groups[number + 2 :] = [rest[n : n + tall] for n in range(0, rest.shape[0], tall)]
        groups[number] = x * lax.rsqrt(pivots)
    return jnp.concatenate(groups)


def orthonormal(total, partner, mine, theirs, mine_first, scale):
    size = total.shape[1]
    tall = 16

    def kernel(first_ref, total_ref, partner_ref, mine_ref, theirs_ref, out_ref):
        rows = lax.broadcasted_iota(jnp.int32, (size, size), 0)
        lanes = lax.broadcasted_iota(jnp.int32, (size, size), 1)
        is_first = first_ref[0] != 0
        cross = jnp.where(is_first, total_ref[:size, :], partner_ref[:size, :])
        both = jnp.where(is_first, partner_ref[:size, :], total_ref[:size, :])
        diagonal = jnp.where(is_first, partner_ref[size : size + 1, :], total_ref[size : size + 1, :])
        mirrored = both.T
        first = factor(jnp.where(rows >= lanes, both, mirrored), tall)
        first = jnp.where(rows >= lanes, first, 0.0)
        below = exact_dot(cross, first, ((1,), (1,)))
        second = jnp.where(lanes > rows, both, mirrored)
        second = jnp.where(lanes == rows, diagonal, second)
        last = factor(second - exact_dot(below, below, ((1,), (1,))), tall)
        last = jnp.where(rows >= lanes, last, 0.0)
        left = jnp.where(is_first, mine_ref[...], theirs_ref[...])
        left = exact_dot(left, first, ((1,), (1,)))
        out_ref[:, :size] = scale * left
        right = jnp.where(is_first, theirs_ref[...], mine_ref[...]) - exact_dot(left, below, ((1,), (1,)))
        out_ref[:, size:] = scale * exact_dot(right, last, ((1,), (1,)))

    vmem = pl.BlockSpec(memory_space=pltpu.VMEM)
    return pl.pallas_call(
        kernel,
        in_specs=[pl.BlockSpec(memory_space=pltpu.SMEM), vmem, vmem, vmem, vmem],
        out_specs=vmem,
        out_shape=jax.ShapeDtypeStruct((mine.shape[0], 2 * size), jnp.float32),
        compiler_params=pltpu.CompilerParams(vmem_limit_bytes=8 << 20),
    )(mine_first.astype(jnp.int32).reshape(1), total, partner, mine, theirs)


def on_device(blocks, col_index, vectors):
    center, scales, carries = filter_coefs(DEGREE)
    row_count = lax.axis_size("row")
    col_count = lax.axis_size("col")
    row_rank = lax.axis_index("row")
    col_rank = lax.axis_index("col")
    core = col_rank % 2
    group_rows, _, width, _ = blocks.shape
    piece_rows, states = vectors.shape
    half = states // 2
    tile_blocks = piece_rows // width * row_count
    tile_rows = tile_blocks * width
    row_bits = bits_below(row_count)
    z_count = col_count // 2
    z_bits = [2 * bit for bit in bits_below(z_count)]
    narrow = jnp.bfloat16

    mine_first = core == 0

    def kept_and_sent(value):
        left, right = value[:, :half], value[:, half:]
        return jnp.where(mine_first, left, right), jnp.where(mine_first, right, left)

    low_start = vectors.astype(narrow)
    arrived = {0: low_start, **{k: swap(low_start, "row", k) for k in partners(row_count)}}
    low_own, sent = kept_and_sent(in_order(arrived, row_rank))
    low_other = swap(sent, "col", 1)
    own_start, sent = kept_and_sent(vectors)
    other_start = swap(sent, "col", 1)

    own = densify(blocks, col_index, tile_blocks)
    other = swap(own, "col", 1)

    first_row = row_rank * group_rows
    own_offset = first_row - col_rank * tile_blocks
    other_offset = first_row - (col_rank ^ 1) * tile_blocks

    segments = group_rows // tile_blocks

    def spread(low, offset):
        value = low.astype(jnp.float32)
        return jnp.concatenate(
            [jnp.where(offset == -k * tile_blocks, value, 0.0) for k in range(segments)]
        )

    def picked(low, offset):
        value = low.astype(jnp.float32).reshape(segments, tile_rows, half)
        parts = [jnp.where(offset == -k * tile_blocks, value[k], 0.0) for k in range(segments)]
        return sum(parts[1:], parts[0])

    def forward(low_own, low_other):
        middle = group_rows * width // 2
        shifted = center * (spread(low_own, own_offset) + spread(low_other, other_offset))

        def part(rows):
            product = jnp.dot(own[rows], low_own, preferred_element_type=jnp.float32)
            product = product + jnp.dot(other[rows], low_other, preferred_element_type=jnp.float32)
            return product - shifted[rows]

        return part(slice(0, middle)), part(slice(middle, None))

    def backward(low):
        def part(tile, offset):
            product = lax.dot_general(tile, low, (((0,), (0,)), ((), ())), preferred_element_type=jnp.float32)
            return product - center * picked(low, offset)

        return part(own, own_offset), part(other, other_offset)

    def sum_over(axis, bits, one, two):
        for level, (bit_one, bit_two) in enumerate(zip(bits, reversed(bits))):
            from_one = swap(one.astype(narrow), axis, bit_one)
            from_two = swap(two.astype(narrow), axis, bit_two)
            if level < len(bits) - 1:
                from_one, from_two = lax.optimization_barrier((from_one, from_two))
            one, two = one + from_one.astype(jnp.float32), two + from_two.astype(jnp.float32)
        return one, two

    def placed(piece):
        here = jnp.arange(row_count)[:, None, None] == row_rank
        return jnp.where(here, piece[None], 0.0).reshape(tile_rows, half)

    y1_one, y1_two = [
        scales[0] * image for image in sum_over("col", z_bits, *forward(low_own, low_other))
    ]
    part_own, part_other = backward(jnp.concatenate([y1_one.astype(narrow), y1_two.astype(narrow)]))
    y2_own, y2_other = sum_over(
        "row",
        row_bits,
        scales[1] * part_own - carries[1] * placed(own_start),
        scales[1] * part_other - carries[1] * placed(other_start),
    )
    image_one, image_two = sum_over(
        "col", z_bits, *forward(y2_own.astype(narrow), y2_other.astype(narrow))
    )
    low_one = (scales[2] * image_one - carries[2] * y1_one).astype(narrow)
    low_two = (scales[2] * image_two - carries[2] * y1_two).astype(narrow)
    part_own, part_other = backward(jnp.concatenate([low_one, low_two]))
    image_own, image_other = sum_over("row", row_bits, part_own, part_other)
    y4_own = scales[3] * image_own - carries[3] * y2_own
    y4_other = scales[3] * image_other - carries[3] * y2_other

    theirs_own = swap(y4_other, "col", 1)
    theirs_other = swap(y4_own, "col", 1)

    def product(left, right):
        return exact_dot(left, right, ((0,), (0,)))

    corner = product(y4_own, y4_own) + product(y4_other, y4_other)
    cross = product(theirs_own, jnp.where(mine_first, y4_own, theirs_own))
    cross = cross + product(theirs_other, jnp.where(mine_first, y4_other, theirs_other))
    rows = lax.broadcasted_iota(jnp.int32, (half, half), 0)
    lanes = lax.broadcasted_iota(jnp.int32, (half, half), 1)
    packed = jnp.where(mine_first | (rows >= lanes), cross, corner)
    diagonal = jnp.sum(jnp.where(rows == lanes, corner, 0.0), axis=0, keepdims=True)
    total = jnp.concatenate([packed, jnp.pad(diagonal, ((0, 7), (0, 0)))])
    total = sum([swap(total, "col", 2 * k) for k in partners(z_count)], total)
    partner = swap(total, "col", 1)
    orbital_count = piece_rows * row_count * col_count
    here = row_rank * piece_rows
    mine = lax.dynamic_slice_in_dim(y4_own, here, piece_rows, 0)
    theirs = lax.dynamic_slice_in_dim(theirs_own, here, piece_rows, 0)
    return orthonormal(total, partner, mine, theirs, mine_first, math.sqrt(orbital_count))


def solution(mesh):
    return jax.shard_map(
        on_device,
        mesh=mesh,
        in_specs=(P("row", "col", None, None), P("row", "col"), P(("col", "row"), None)),
        out_specs=P(("col", "row"), None),
        check_vma=False,
    )
```

```python
import math

import jax
import jax.numpy as jnp
from jax import lax
from jax.experimental import pallas as pl
from jax.experimental.pallas import tpu as pltpu
from jax.sharding import PartitionSpec as P

DEGREE = 4


LOWER = -2.0
CUTOFF = 0.0
UPPER = 2.0


def filter_coefs(degree):
    half_width = (UPPER - CUTOFF) / 2.0
    center = (UPPER + CUTOFF) / 2.0
    sigma_now = half_width / (LOWER - center)
    tau_value = 2.0 / sigma_now
    scales = [sigma_now / half_width]
    carries = [0.0]
    for number in range(1, degree):
        sigma_next = 1.0 / (tau_value - sigma_now)
        scales.append(2.0 * sigma_next / half_width)
        carries.append(sigma_now * sigma_next)
        sigma_now = sigma_next
    return (center, scales, carries)


def swap(value, axis, distance):
    count = lax.axis_size(axis)
    return lax.ppermute(value, axis, [(i, i ^ distance) for i in range(count)])


def bits_below(count):
    return [1 << n for n in range(count.bit_length() - 1)]


def partners(count):
    return [1, *range(count - 1, 1, -1)]


def in_order(values, rank):
    stacked = jnp.stack(list(values.values()))

    def value_of(index):
        place = rank ^ index
        for number, distance in enumerate(values):
            if number != distance:
                place = jnp.where((rank ^ index) == distance, number, place)
        return lax.dynamic_index_in_dim(stacked, place, 0, False)

    return jnp.concatenate([value_of(index) for index in range(len(values))])


def densify(blocks, col_index, tile_blocks):
    group_rows, slots, width, _ = blocks.shape
    slots = min(slots, tile_blocks)
    step = max(group_rows // 2, 1)

    def kernel(index_ref, blocks_ref, tile_ref):
        nothing = jnp.zeros((width, width), blocks.dtype)
        for inner in range(step):
            places = [index_ref[pl.program_id(0) * step + inner, slot] for slot in range(slots)]
            places = [jnp.where(place >= 0, lax.rem(place, tile_blocks), -1) for place in places]
            for column in range(tile_blocks):
                value = nothing
                for slot in range(slots):
                    value = jnp.where(places[slot] == column, blocks_ref[inner, slot], value)
                tile_ref[inner * width : (inner + 1) * width, column * width : (column + 1) * width] = value

    return pl.pallas_call(
        kernel,
        grid_spec=pltpu.PrefetchScalarGridSpec(
            num_scalar_prefetch=1,
            grid=(group_rows // step,),
            in_specs=[pl.BlockSpec((step, slots, width, width), lambda i, index: (i, 0, 0, 0))],
            out_specs=pl.BlockSpec((step * width, tile_blocks * width), lambda i, index: (i, 0)),
        ),
        out_shape=jax.ShapeDtypeStruct((group_rows * width, tile_blocks * width), blocks.dtype),
        compiler_params=pltpu.CompilerParams(vmem_limit_bytes=24 << 20),
    )(col_index, blocks)


def exact_dot(a, b, dims):
    return lax.dot_general(
        a, b, (dims, ((), ())), precision=lax.Precision.HIGHEST, preferred_element_type=jnp.float32
    )


def tree_sum(terms):
    while len(terms) > 1:
        terms = [sum(terms[n + 1 : n + 2], terms[n]) for n in range(0, len(terms), 2)]
    return terms[0]


def factor(matrix, tall):
    size = matrix.shape[1]
    groups = [matrix[first : first + tall] for first in range(0, size, tall)]
    sub = lax.broadcasted_iota(jnp.int32, (tall, size), 0)
    lane = lax.broadcasted_iota(jnp.int32, (tall, size), 1)
    for number, head in enumerate(groups):
        first = tall * number
        block = (lane >= first) & (lane < first + tall)
        columns = [jnp.broadcast_to(head[:, first + q : first + q + 1], head.shape) for q in range(tall)]
        x = jnp.where(block, jnp.where(lane - first == sub, 1.0, 0.0), head)
        z = x
        pivots = jnp.ones_like(x)
        inverses = jnp.ones_like(x)
        for p in range(tall):
            pivot = columns[p][p : p + 1, :]
            inverse = 1.0 / pivot
            masked = jnp.where(sub == p, 0.0, columns[p])
            others = masked * inverse
            below = jnp.where(sub > p, others, 0.0)
            for q in range(p + 1, tall):
                if q == p + 1:
                    columns[q] = columns[q] - (masked * columns[q][p : p + 1, :]) * inverse
                else:
                    columns[q] = columns[q] - others * columns[q][p : p + 1, :]
            x = x - below * x[p : p + 1, :]
            z = z - others * z[p : p + 1, :]
            pivots = jnp.where(sub == p, pivot, pivots)
            inverses = jnp.where(sub == p, inverse, inverses)
        z = z * inverses
        if number + 1 < len(groups):
            following = groups[number + 1]
            terms = [following[:, first + p : first + p + 1] * z[p : p + 1, :] for p in range(tall)]
            groups[number + 1] = jnp.where(block, 0.0, following) - tree_sum(terms)
        if number + 2 < len(groups):
            rest = jnp.concatenate(groups[number + 2 :])
            lanes = lax.broadcasted_iota(jnp.int32, rest.shape, 1)
            gone = (lanes >= first) & (lanes < first + tall)
            placed = [jnp.zeros((first, size), jnp.float32)] if first else []
            placed = jnp.concatenate([*placed, z, jnp.zeros((size - first - tall, size), jnp.float32)])
            rest = jnp.where(gone, 0.0, rest) - exact_dot(rest, placed, ((1,), (0,)))
            groups[number + 2 :] = [rest[n : n + tall] for n in range(0, rest.shape[0], tall)]
        groups[number] = x * lax.rsqrt(pivots)
    return jnp.concatenate(groups)


def orthonormal(total, partner, mine, theirs, mine_first, scale):
    size = total.shape[1]
    tall = 16

    def kernel(first_ref, total_ref, partner_ref, mine_ref, theirs_ref, out_ref):
        rows = lax.broadcasted_iota(jnp.int32, (size, size), 0)
        lanes = lax.broadcasted_iota(jnp.int32, (size, size), 1)
        is_first = first_ref[0] != 0
        cross = jnp.where(is_first, total_ref[:size, :], partner_ref[:size, :])
        both = jnp.where(is_first, partner_ref[:size, :], total_ref[:size, :])
        diagonal = jnp.where(is_first, partner_ref[size : size + 1, :], total_ref[size : size + 1, :])
        mirrored = both.T
        first = factor(jnp.where(rows >= lanes, both, mirrored), tall)
        first = jnp.where(rows >= lanes, first, 0.0)
        below = exact_dot(cross, first, ((1,), (1,)))
        second = jnp.where(lanes > rows, both, mirrored)
        second = jnp.where(lanes == rows, diagonal, second)
        last = factor(second - exact_dot(below, below, ((1,), (1,))), tall)
        last = jnp.where(rows >= lanes, last, 0.0)
        left = jnp.where(is_first, mine_ref[...], theirs_ref[...])
        left = exact_dot(left, first, ((1,), (1,)))
        out_ref[:, :size] = scale * left
        right = jnp.where(is_first, theirs_ref[...], mine_ref[...]) - exact_dot(left, below, ((1,), (1,)))
        out_ref[:, size:] = scale * exact_dot(right, last, ((1,), (1,)))

    vmem = pl.BlockSpec(memory_space=pltpu.VMEM)
    return pl.pallas_call(
        kernel,
        in_specs=[pl.BlockSpec(memory_space=pltpu.SMEM), vmem, vmem, vmem, vmem],
        out_specs=vmem,
        out_shape=jax.ShapeDtypeStruct((mine.shape[0], 2 * size), jnp.float32),
        compiler_params=pltpu.CompilerParams(vmem_limit_bytes=8 << 20),
    )(mine_first.astype(jnp.int32).reshape(1), total, partner, mine, theirs)


def on_device(blocks, col_index, vectors):
    center, scales, carries = filter_coefs(DEGREE)
    row_count = lax.axis_size("row")
    col_count = lax.axis_size("col")
    row_rank = lax.axis_index("row")
    col_rank = lax.axis_index("col")
    core = col_rank % 2
    group_rows, _, width, _ = blocks.shape
    piece_rows, states = vectors.shape
    half = states // 2
    tile_blocks = piece_rows // width * row_count
    tile_rows = tile_blocks * width
    row_bits = bits_below(row_count)
    z_count = col_count // 2
    z_bits = [2 * bit for bit in bits_below(z_count)]
    narrow = jnp.bfloat16

    mine_first = core == 0

    def kept_and_sent(value):
        left, right = value[:, :half], value[:, half:]
        return jnp.where(mine_first, left, right), jnp.where(mine_first, right, left)

    low_start = vectors.astype(narrow)
    arrived = {0: low_start, **{k: swap(low_start, "row", k) for k in partners(row_count)}}
    low_own, sent = kept_and_sent(in_order(arrived, row_rank))
    low_other = swap(sent, "col", 1)
    own_start, sent = kept_and_sent(vectors)
    other_start = swap(sent, "col", 1)

    own = densify(blocks, col_index, tile_blocks)
    other = swap(own, "col", 1)

    first_row = row_rank * group_rows
    own_offset = first_row - col_rank * tile_blocks
    other_offset = first_row - (col_rank ^ 1) * tile_blocks

    segments = group_rows // tile_blocks

    def spread(low, offset):
        value = low.astype(jnp.float32)
        return jnp.concatenate(
            [jnp.where(offset == -k * tile_blocks, value, 0.0) for k in range(segments)]
        )

    def picked(low, offset):
        value = low.astype(jnp.float32).reshape(segments, tile_rows, half)
        parts = [jnp.where(offset == -k * tile_blocks, value[k], 0.0) for k in range(segments)]
        return sum(parts[1:], parts[0])

    def forward(low_own, low_other):
        product = jnp.dot(own, low_own, preferred_element_type=jnp.float32)
        product = product + jnp.dot(other, low_other, preferred_element_type=jnp.float32)
        product = product - center * (spread(low_own, own_offset) + spread(low_other, other_offset))
        middle = product.shape[0] // 2
        return product[:middle], product[middle:]

    def backward(low):
        def part(tile, offset):
            product = lax.dot_general(tile, low, (((0,), (0,)), ((), ())), preferred_element_type=jnp.float32)
            return product - center * picked(low, offset)

        return part(own, own_offset), part(other, other_offset)

    def sum_over(axis, bits, one, two):
        for bit_one, bit_two in zip(bits, reversed(bits)):
            sent = [(one.astype(narrow), bit_one), (two.astype(narrow), bit_two)]
            if bit_two > bit_one:
                from_two, from_one = lax.optimization_barrier(
                    tuple(swap(value, axis, bit) for value, bit in reversed(sent))
                )
            else:
                from_one, from_two = lax.optimization_barrier(
                    tuple(swap(value, axis, bit) for value, bit in sent)
                )
            one, two = one + from_one.astype(jnp.float32), two + from_two.astype(jnp.float32)
        return one, two

    def placed(piece):
        here = jnp.arange(row_count)[:, None, None] == row_rank
        return jnp.where(here, piece[None], 0.0).reshape(tile_rows, half)

    y1_one, y1_two = [
        scales[0] * image for image in sum_over("col", z_bits, *forward(low_own, low_other))
    ]
    part_own, part_other = backward(jnp.concatenate([y1_one.astype(narrow), y1_two.astype(narrow)]))
    y2_own, y2_other = sum_over(
        "row",
        row_bits,
        scales[1] * part_own - carries[1] * placed(own_start),
        scales[1] * part_other - carries[1] * placed(other_start),
    )
    image_one, image_two = sum_over(
        "col", z_bits, *forward(y2_own.astype(narrow), y2_other.astype(narrow))
    )
    low_one = (scales[2] * image_one - carries[2] * y1_one).astype(narrow)
    low_two = (scales[2] * image_two - carries[2] * y1_two).astype(narrow)
    part_own, part_other = backward(jnp.concatenate([low_one, low_two]))
    image_own, image_other = sum_over("row", row_bits, part_own, part_other)
    y4_own = scales[3] * image_own - carries[3] * y2_own
    y4_other = scales[3] * image_other - carries[3] * y2_other

    mine = jnp.concatenate([y4_own, y4_other])
    theirs = swap(jnp.concatenate([y4_other, y4_own]), "col", 1)
    corner = exact_dot(mine, mine, ((0,), (0,)))
    cross = exact_dot(theirs, jnp.where(mine_first, mine, theirs), ((0,), (0,)))
    rows = lax.broadcasted_iota(jnp.int32, (half, half), 0)
    lanes = lax.broadcasted_iota(jnp.int32, (half, half), 1)
    packed = jnp.where(mine_first | (rows >= lanes), cross, corner)
    diagonal = jnp.sum(jnp.where(rows == lanes, corner, 0.0), axis=0, keepdims=True)
    total = jnp.concatenate([packed, jnp.pad(diagonal, ((0, 7), (0, 0)))])
    total = sum([swap(total, "col", 2 * k) for k in partners(z_count)], total)
    partner = swap(total, "col", 1)
    orbital_count = piece_rows * row_count * col_count
    here = row_rank * piece_rows
    mine = lax.dynamic_slice_in_dim(mine, here, piece_rows, 0)
    theirs = lax.dynamic_slice_in_dim(theirs, here, piece_rows, 0)
    return orthonormal(total, partner, mine, theirs, mine_first, math.sqrt(orbital_count))


def solution(mesh):
    return jax.shard_map(
        on_device,
        mesh=mesh,
        in_specs=(P("row", "col", None, None), P("row", "col"), P(("col", "row"), None)),
        out_specs=P(("col", "row"), None),
        check_vma=False,
    )
```

```python
import math

import jax
import jax.numpy as jnp
from jax import lax
from jax.experimental import pallas as pl
from jax.experimental.pallas import tpu as pltpu
from jax.sharding import PartitionSpec as P

DEGREE = 4


LOWER = -2.0
CUTOFF = 0.0
UPPER = 2.0


def filter_coefs(degree):
    half_width = (UPPER - CUTOFF) / 2.0
    center = (UPPER + CUTOFF) / 2.0
    sigma_now = half_width / (LOWER - center)
    tau_value = 2.0 / sigma_now
    scales = [sigma_now / half_width]
    carries = [0.0]
    for number in range(1, degree):
        sigma_next = 1.0 / (tau_value - sigma_now)
        scales.append(2.0 * sigma_next / half_width)
        carries.append(sigma_now * sigma_next)
        sigma_now = sigma_next
    return (center, scales, carries)


def swap(value, axis, distance):
    count = lax.axis_size(axis)
    return lax.ppermute(value, axis, [(i, i ^ distance) for i in range(count)])


def bits_below(count):
    return [1 << n for n in range(count.bit_length() - 1)]


def partners(count):
    return [1, *range(count - 1, 1, -1)]


def in_order(values, rank):
    stacked = jnp.stack(list(values.values()))

    def value_of(index):
        place = rank ^ index
        for number, distance in enumerate(values):
            if number != distance:
                place = jnp.where((rank ^ index) == distance, number, place)
        return lax.dynamic_index_in_dim(stacked, place, 0, False)

    return jnp.concatenate([value_of(index) for index in range(len(values))])


def densify(blocks, col_index, tile_blocks):
    group_rows, slots, width, _ = blocks.shape
    slots = min(slots, tile_blocks)
    step = max(group_rows // 2, 1)

    def kernel(index_ref, blocks_ref, tile_ref):
        nothing = jnp.zeros((width, width), blocks.dtype)
        for inner in range(step):
            places = [index_ref[pl.program_id(0) * step + inner, slot] for slot in range(slots)]
            places = [jnp.where(place >= 0, lax.rem(place, tile_blocks), -1) for place in places]
            for column in range(tile_blocks):
                value = nothing
                for slot in range(slots):
                    value = jnp.where(places[slot] == column, blocks_ref[inner, slot], value)
                tile_ref[inner * width : (inner + 1) * width, column * width : (column + 1) * width] = value

    return pl.pallas_call(
        kernel,
        grid_spec=pltpu.PrefetchScalarGridSpec(
            num_scalar_prefetch=1,
            grid=(group_rows // step,),
            in_specs=[pl.BlockSpec((step, slots, width, width), lambda i, index: (i, 0, 0, 0))],
            out_specs=pl.BlockSpec((step * width, tile_blocks * width), lambda i, index: (i, 0)),
        ),
        out_shape=jax.ShapeDtypeStruct((group_rows * width, tile_blocks * width), blocks.dtype),
        compiler_params=pltpu.CompilerParams(vmem_limit_bytes=24 << 20),
    )(col_index, blocks)


def exact_dot(a, b, dims):
    return lax.dot_general(
        a, b, (dims, ((), ())), precision=lax.Precision.HIGHEST, preferred_element_type=jnp.float32
    )


def tree_sum(terms):
    while len(terms) > 1:
        terms = [sum(terms[n + 1 : n + 2], terms[n]) for n in range(0, len(terms), 2)]
    return terms[0]


def factor(matrix, tall):
    size = matrix.shape[1]
    groups = [matrix[first : first + tall] for first in range(0, size, tall)]
    sub = lax.broadcasted_iota(jnp.int32, (tall, size), 0)
    lane = lax.broadcasted_iota(jnp.int32, (tall, size), 1)
    for number, head in enumerate(groups):
        first = tall * number
        block = (lane >= first) & (lane < first + tall)
        columns = [jnp.broadcast_to(head[:, first + q : first + q + 1], head.shape) for q in range(tall)]
        x = jnp.where(block, jnp.where(lane - first == sub, 1.0, 0.0), head)
        z = x
        pivots = jnp.ones_like(x)
        inverses = jnp.ones_like(x)
        for p in range(tall):
            pivot = columns[p][p : p + 1, :]
            inverse = 1.0 / pivot
            masked = jnp.where(sub == p, 0.0, columns[p])
            others = masked * inverse
            below = jnp.where(sub > p, others, 0.0)
            for q in range(p + 1, tall):
                if q == p + 1:
                    columns[q] = columns[q] - (masked * columns[q][p : p + 1, :]) * inverse
                else:
                    columns[q] = columns[q] - others * columns[q][p : p + 1, :]
            x = x - below * x[p : p + 1, :]
            z = z - others * z[p : p + 1, :]
            pivots = jnp.where(sub == p, pivot, pivots)
            inverses = jnp.where(sub == p, inverse, inverses)
        z = z * inverses
        if number + 1 < len(groups):
            following = groups[number + 1]
            terms = [following[:, first + p : first + p + 1] * z[p : p + 1, :] for p in range(tall)]
            groups[number + 1] = jnp.where(block, 0.0, following) - tree_sum(terms)
        if number + 2 < len(groups):
            rest = jnp.concatenate(groups[number + 2 :])
            lanes = lax.broadcasted_iota(jnp.int32, rest.shape, 1)
            gone = (lanes >= first) & (lanes < first + tall)
            placed = [jnp.zeros((first, size), jnp.float32)] if first else []
            placed = jnp.concatenate([*placed, z, jnp.zeros((size - first - tall, size), jnp.float32)])
            rest = jnp.where(gone, 0.0, rest) - exact_dot(rest, placed, ((1,), (0,)))
            groups[number + 2 :] = [rest[n : n + tall] for n in range(0, rest.shape[0], tall)]
        groups[number] = x * lax.rsqrt(pivots)
    return jnp.concatenate(groups)


def orthonormal(total, partner, mine, theirs, mine_first, scale):
    size = total.shape[1]
    tall = 16

    def kernel(first_ref, total_ref, partner_ref, mine_ref, theirs_ref, out_ref):
        rows = lax.broadcasted_iota(jnp.int32, (size, size), 0)
        lanes = lax.broadcasted_iota(jnp.int32, (size, size), 1)
        is_first = first_ref[0] != 0
        cross = jnp.where(is_first, total_ref[:size, :], partner_ref[:size, :])
        both = jnp.where(is_first, partner_ref[:size, :], total_ref[:size, :])
        diagonal = jnp.where(is_first, partner_ref[size : size + 1, :], total_ref[size : size + 1, :])
        mirrored = both.T
        first = factor(jnp.where(rows >= lanes, both, mirrored), tall)
        first = jnp.where(rows >= lanes, first, 0.0)
        below = exact_dot(cross, first, ((1,), (1,)))
        second = jnp.where(lanes > rows, both, mirrored)
        second = jnp.where(lanes == rows, diagonal, second)
        last = factor(second - exact_dot(below, below, ((1,), (1,))), tall)
        last = jnp.where(rows >= lanes, last, 0.0)
        left = jnp.where(is_first, mine_ref[...], theirs_ref[...])
        left = exact_dot(left, first, ((1,), (1,)))
        out_ref[:, :size] = scale * left
        right = jnp.where(is_first, theirs_ref[...], mine_ref[...]) - exact_dot(left, below, ((1,), (1,)))
        out_ref[:, size:] = scale * exact_dot(right, last, ((1,), (1,)))

    vmem = pl.BlockSpec(memory_space=pltpu.VMEM)
    return pl.pallas_call(
        kernel,
        in_specs=[pl.BlockSpec(memory_space=pltpu.SMEM), vmem, vmem, vmem, vmem],
        out_specs=vmem,
        out_shape=jax.ShapeDtypeStruct((mine.shape[0], 2 * size), jnp.float32),
        compiler_params=pltpu.CompilerParams(vmem_limit_bytes=8 << 20),
    )(mine_first.astype(jnp.int32).reshape(1), total, partner, mine, theirs)


def on_device(blocks, col_index, vectors):
    center, scales, carries = filter_coefs(DEGREE)
    row_count = lax.axis_size("row")
    col_count = lax.axis_size("col")
    row_rank = lax.axis_index("row")
    col_rank = lax.axis_index("col")
    core = col_rank % 2
    group_rows, _, width, _ = blocks.shape
    piece_rows, states = vectors.shape
    half = states // 2
    tile_blocks = piece_rows // width * row_count
    tile_rows = tile_blocks * width
    row_bits = bits_below(row_count)
    z_count = col_count // 2
    z_bits = [2 * bit for bit in bits_below(z_count)]
    narrow = jnp.bfloat16

    mine_first = core == 0

    def kept_and_sent(value):
        left, right = value[:, :half], value[:, half:]
        return jnp.where(mine_first, left, right), jnp.where(mine_first, right, left)

    low_start = vectors.astype(narrow)
    arrived = {0: low_start, **{k: swap(low_start, "row", k) for k in partners(row_count)}}
    low_group = in_order(arrived, row_rank)
    own_start, sent = kept_and_sent(vectors)
    other_start = swap(sent, "col", 1)

    own = densify(blocks, col_index, tile_blocks)

    first_row = row_rank * group_rows
    own_offset = first_row - col_rank * tile_blocks
    other_offset = first_row - (col_rank ^ 1) * tile_blocks

    segments = group_rows // tile_blocks

    def spread(low, offset):
        value = low.astype(jnp.float32)
        return jnp.concatenate(
            [jnp.where(offset == -k * tile_blocks, value, 0.0) for k in range(segments)]
        )

    def picked(low, offset):
        value = low.astype(jnp.float32).reshape(segments, tile_rows, low.shape[1])
        parts = [jnp.where(offset == -k * tile_blocks, value[k], 0.0) for k in range(segments)]
        return sum(parts[1:], parts[0])

    def halves(value):
        middle = value.shape[0] // 2
        return value[:middle], value[middle:]

    def part_of(tile, low, offset):
        product = jnp.dot(tile, low, preferred_element_type=jnp.float32)
        return product - center * spread(low, offset)

    def backward(low, own, other):
        def part(tile, offset):
            product = lax.dot_general(tile, low, (((0,), (0,)), ((), ())), preferred_element_type=jnp.float32)
            return product - center * picked(low, offset)

        return part(own, own_offset), part(other, other_offset)

    def sum_over(axis, bits, one, two):
        for bit_one, bit_two in zip(bits, reversed(bits)):
            sent = [(one.astype(narrow), bit_one), (two.astype(narrow), bit_two)]
            if bit_two > bit_one:
                from_two, from_one = lax.optimization_barrier(
                    tuple(swap(value, axis, bit) for value, bit in reversed(sent))
                )
            else:
                from_one, from_two = lax.optimization_barrier(
                    tuple(swap(value, axis, bit) for value, bit in sent)
                )
            one, two = one + from_one.astype(jnp.float32), two + from_two.astype(jnp.float32)
        return one, two

    def placed(piece):
        here = jnp.arange(row_count)[:, None, None] == row_rank
        return jnp.where(here, piece[None], 0.0).reshape(tile_rows, half)

    kept, sent = kept_and_sent(part_of(own, low_group, own_offset))
    image = kept + swap(sent.astype(narrow), "col", 1).astype(jnp.float32)
    y1_one, y1_two = [scales[0] * image for image in sum_over("col", z_bits, *halves(image))]
    own, _ = lax.optimization_barrier((own, image))
    other = swap(own, "col", 1)
    part_own, part_other = backward(
        jnp.concatenate([y1_one.astype(narrow), y1_two.astype(narrow)]), own, other
    )
    y2_own, y2_other = sum_over(
        "row",
        row_bits,
        scales[1] * part_own - carries[1] * placed(own_start),
        scales[1] * part_other - carries[1] * placed(other_start),
    )
    image_one, image_two = sum_over(
        "col",
        z_bits,
        *halves(
            part_of(own, y2_own.astype(narrow), own_offset)
            + part_of(other, y2_other.astype(narrow), other_offset)
        ),
    )
    low_one = (scales[2] * image_one - carries[2] * y1_one).astype(narrow)
    low_two = (scales[2] * image_two - carries[2] * y1_two).astype(narrow)
    part_own, part_other = backward(jnp.concatenate([low_one, low_two]), own, other)
    image_own, image_other = sum_over("row", row_bits, part_own, part_other)
    y4_own = scales[3] * image_own - carries[3] * y2_own
    y4_other = scales[3] * image_other - carries[3] * y2_other

    mine = jnp.concatenate([y4_own, y4_other])
    theirs = swap(jnp.concatenate([y4_other, y4_own]).astype(narrow), "col", 1).astype(jnp.float32)
    corner = exact_dot(mine, mine, ((0,), (0,)))
    cross = exact_dot(theirs, jnp.where(mine_first, mine, theirs), ((0,), (0,)))
    rows = lax.broadcasted_iota(jnp.int32, (half, half), 0)
    lanes = lax.broadcasted_iota(jnp.int32, (half, half), 1)
    packed = jnp.where(mine_first | (rows >= lanes), cross, corner)
    diagonal = jnp.sum(jnp.where(rows == lanes, corner, 0.0), axis=0, keepdims=True)
    total = jnp.concatenate([packed, jnp.pad(diagonal, ((0, 7), (0, 0)))])
    total = sum([swap(total, "col", 2 * k) for k in partners(z_count)], total)
    partner = swap(total, "col", 1)
    orbital_count = piece_rows * row_count * col_count
    here = row_rank * piece_rows
    mine = lax.dynamic_slice_in_dim(mine, here, piece_rows, 0)
    theirs = lax.dynamic_slice_in_dim(theirs, here, piece_rows, 0)
    return orthonormal(total, partner, mine, theirs, mine_first, math.sqrt(orbital_count))


def solution(mesh):
    return jax.shard_map(
        on_device,
        mesh=mesh,
        in_specs=(P("row", "col", None, None), P("row", "col"), P(("col", "row"), None)),
        out_specs=P(("col", "row"), None),
        check_vma=False,
    )
```

```python
import math

import jax
import jax.numpy as jnp
from jax import lax
from jax.experimental import pallas as pl
from jax.experimental.pallas import tpu as pltpu
from jax.sharding import PartitionSpec as P

DEGREE = 4


LOWER = -2.0
CUTOFF = 0.0
UPPER = 2.0


def filter_coefs(degree):
    half_width = (UPPER - CUTOFF) / 2.0
    center = (UPPER + CUTOFF) / 2.0
    sigma_now = half_width / (LOWER - center)
    tau_value = 2.0 / sigma_now
    scales = [sigma_now / half_width]
    carries = [0.0]
    for number in range(1, degree):
        sigma_next = 1.0 / (tau_value - sigma_now)
        scales.append(2.0 * sigma_next / half_width)
        carries.append(sigma_now * sigma_next)
        sigma_now = sigma_next
    return (center, scales, carries)


def swap(value, axis, distance):
    count = lax.axis_size(axis)
    return lax.ppermute(value, axis, [(i, i ^ distance) for i in range(count)])


def bits_below(count):
    return [1 << n for n in range(count.bit_length() - 1)]


def partners(count):
    return [1, *range(count - 1, 1, -1)]


def in_order(values, rank):
    stacked = jnp.stack(list(values.values()))

    def value_of(index):
        place = rank ^ index
        for number, distance in enumerate(values):
            if number != distance:
                place = jnp.where((rank ^ index) == distance, number, place)
        return lax.dynamic_index_in_dim(stacked, place, 0, False)

    return jnp.concatenate([value_of(index) for index in range(len(values))])


def densify(blocks, col_index, tile_blocks):
    group_rows, slots, width, _ = blocks.shape
    slots = min(slots, tile_blocks)
    step = max(group_rows // 2, 1)

    def kernel(index_ref, blocks_ref, tile_ref):
        nothing = jnp.zeros((width, width), blocks.dtype)
        for inner in range(step):
            places = [index_ref[pl.program_id(0) * step + inner, slot] for slot in range(slots)]
            places = [jnp.where(place >= 0, lax.rem(place, tile_blocks), -1) for place in places]
            for column in range(tile_blocks):
                value = nothing
                for slot in range(slots):
                    value = jnp.where(places[slot] == column, blocks_ref[inner, slot], value)
                tile_ref[inner * width : (inner + 1) * width, column * width : (column + 1) * width] = value

    return pl.pallas_call(
        kernel,
        grid_spec=pltpu.PrefetchScalarGridSpec(
            num_scalar_prefetch=1,
            grid=(group_rows // step,),
            in_specs=[pl.BlockSpec((step, slots, width, width), lambda i, index: (i, 0, 0, 0))],
            out_specs=pl.BlockSpec((step * width, tile_blocks * width), lambda i, index: (i, 0)),
        ),
        out_shape=jax.ShapeDtypeStruct((group_rows * width, tile_blocks * width), blocks.dtype),
        compiler_params=pltpu.CompilerParams(vmem_limit_bytes=24 << 20),
    )(col_index, blocks)


def exact_dot(a, b, dims):
    return lax.dot_general(
        a, b, (dims, ((), ())), precision=lax.Precision.HIGHEST, preferred_element_type=jnp.float32
    )


def tree_sum(terms):
    while len(terms) > 1:
        terms = [sum(terms[n + 1 : n + 2], terms[n]) for n in range(0, len(terms), 2)]
    return terms[0]


def factor(matrix, tall):
    size = matrix.shape[1]
    groups = [matrix[first : first + tall] for first in range(0, size, tall)]
    sub = lax.broadcasted_iota(jnp.int32, (tall, size), 0)
    lane = lax.broadcasted_iota(jnp.int32, (tall, size), 1)
    for number, head in enumerate(groups):
        first = tall * number
        block = (lane >= first) & (lane < first + tall)
        columns = [jnp.broadcast_to(head[:, first + q : first + q + 1], head.shape) for q in range(tall)]
        x = jnp.where(block, jnp.where(lane - first == sub, 1.0, 0.0), head)
        z = x
        pivots = jnp.ones_like(x)
        inverses = jnp.ones_like(x)
        for p in range(tall):
            pivot = columns[p][p : p + 1, :]
            inverse = 1.0 / pivot
            masked = jnp.where(sub == p, 0.0, columns[p])
            others = masked * inverse
            below = jnp.where(sub > p, others, 0.0)
            for q in range(p + 1, tall):
                if q == p + 1:
                    columns[q] = columns[q] - (masked * columns[q][p : p + 1, :]) * inverse
                else:
                    columns[q] = columns[q] - others * columns[q][p : p + 1, :]
            x = x - below * x[p : p + 1, :]
            z = z - others * z[p : p + 1, :]
            pivots = jnp.where(sub == p, pivot, pivots)
            inverses = jnp.where(sub == p, inverse, inverses)
        z = z * inverses
        if number + 1 < len(groups):
            following = groups[number + 1]
            terms = [following[:, first + p : first + p + 1] * z[p : p + 1, :] for p in range(tall)]
            groups[number + 1] = jnp.where(block, 0.0, following) - tree_sum(terms)
        if number + 2 < len(groups):
            rest = jnp.concatenate(groups[number + 2 :])
            lanes = lax.broadcasted_iota(jnp.int32, rest.shape, 1)
            gone = (lanes >= first) & (lanes < first + tall)
            placed = [jnp.zeros((first, size), jnp.float32)] if first else []
            placed = jnp.concatenate([*placed, z, jnp.zeros((size - first - tall, size), jnp.float32)])
            rest = jnp.where(gone, 0.0, rest) - exact_dot(rest, placed, ((1,), (0,)))
            groups[number + 2 :] = [rest[n : n + tall] for n in range(0, rest.shape[0], tall)]
        groups[number] = x * lax.rsqrt(pivots)
    return jnp.concatenate(groups)


def orthonormal(total, partner, mine, theirs, mine_first, scale):
    size = total.shape[1]
    tall = 16

    def kernel(first_ref, total_ref, partner_ref, mine_ref, theirs_ref, out_ref):
        rows = lax.broadcasted_iota(jnp.int32, (size, size), 0)
        lanes = lax.broadcasted_iota(jnp.int32, (size, size), 1)
        is_first = first_ref[0] != 0
        cross = jnp.where(is_first, total_ref[:size, :], partner_ref[:size, :])
        both = jnp.where(is_first, partner_ref[:size, :], total_ref[:size, :])
        diagonal = jnp.where(is_first, partner_ref[size : size + 1, :], total_ref[size : size + 1, :])
        mirrored = both.T
        first = factor(jnp.where(rows >= lanes, both, mirrored), tall)
        first = jnp.where(rows >= lanes, first, 0.0)
        below = exact_dot(cross, first, ((1,), (1,)))
        second = jnp.where(lanes > rows, both, mirrored)
        second = jnp.where(lanes == rows, diagonal, second)
        last = factor(second - exact_dot(below, below, ((1,), (1,))), tall)
        last = jnp.where(rows >= lanes, last, 0.0)
        left = jnp.where(is_first, mine_ref[...], theirs_ref[...])
        left = exact_dot(left, first, ((1,), (1,)))
        out_ref[:, :size] = scale * left
        right = jnp.where(is_first, theirs_ref[...], mine_ref[...]) - exact_dot(left, below, ((1,), (1,)))
        out_ref[:, size:] = scale * exact_dot(right, last, ((1,), (1,)))

    vmem = pl.BlockSpec(memory_space=pltpu.VMEM)
    return pl.pallas_call(
        kernel,
        in_specs=[pl.BlockSpec(memory_space=pltpu.SMEM), vmem, vmem, vmem, vmem],
        out_specs=vmem,
        out_shape=jax.ShapeDtypeStruct((mine.shape[0], 2 * size), jnp.float32),
        compiler_params=pltpu.CompilerParams(vmem_limit_bytes=8 << 20),
    )(mine_first.astype(jnp.int32).reshape(1), total, partner, mine, theirs)


def on_device(blocks, col_index, vectors):
    center, scales, carries = filter_coefs(DEGREE)
    row_count = lax.axis_size("row")
    col_count = lax.axis_size("col")
    row_rank = lax.axis_index("row")
    col_rank = lax.axis_index("col")
    core = col_rank % 2
    group_rows, _, width, _ = blocks.shape
    piece_rows, states = vectors.shape
    half = states // 2
    tile_blocks = piece_rows // width * row_count
    tile_rows = tile_blocks * width
    row_bits = bits_below(row_count)
    z_count = col_count // 2
    z_bits = [2 * bit for bit in bits_below(z_count)]
    narrow = jnp.bfloat16

    mine_first = core == 0

    def kept_and_sent(value):
        left, right = value[:, :half], value[:, half:]
        return jnp.where(mine_first, left, right), jnp.where(mine_first, right, left)

    low_start = lax.optimization_barrier(vectors.astype(narrow))
    arrived = {0: low_start, **{k: swap(low_start, "row", k) for k in partners(row_count)}}
    low_group = in_order(arrived, row_rank)
    own_start, sent = kept_and_sent(vectors)
    other_start = swap(sent, "col", 1)

    own = densify(blocks, col_index, tile_blocks)

    first_row = row_rank * group_rows
    own_offset = first_row - col_rank * tile_blocks
    other_offset = first_row - (col_rank ^ 1) * tile_blocks

    segments = group_rows // tile_blocks

    def spread(low, offset):
        value = low.astype(jnp.float32)
        return jnp.concatenate(
            [jnp.where(offset == -k * tile_blocks, value, 0.0) for k in range(segments)]
        )

    def picked(low, offset):
        value = low.astype(jnp.float32).reshape(segments, tile_rows, low.shape[1])
        parts = [jnp.where(offset == -k * tile_blocks, value[k], 0.0) for k in range(segments)]
        return sum(parts[1:], parts[0])

    def halves(value):
        middle = value.shape[0] // 2
        return value[:middle], value[middle:]

    def part_of(tile, low, offset):
        product = jnp.dot(tile, low, preferred_element_type=jnp.float32)
        return product - center * spread(low, offset)

    def backward(low, own, other):
        def part(tile, offset):
            product = lax.dot_general(tile, low, (((0,), (0,)), ((), ())), preferred_element_type=jnp.float32)
            return product - center * picked(low, offset)

        return part(own, own_offset), part(other, other_offset)

    def sum_over(axis, bits, one, two):
        for bit_one, bit_two in zip(bits, reversed(bits)):
            sent = [(one.astype(narrow), bit_one), (two.astype(narrow), bit_two)]
            if bit_two > bit_one:
                from_two, from_one = lax.optimization_barrier(
                    tuple(swap(value, axis, bit) for value, bit in reversed(sent))
                )
            else:
                from_one, from_two = lax.optimization_barrier(
                    tuple(swap(value, axis, bit) for value, bit in sent)
                )
            one, two = one + from_one.astype(jnp.float32), two + from_two.astype(jnp.float32)
        return one, two

    def placed(piece):
        here = jnp.arange(row_count)[:, None, None] == row_rank
        return jnp.where(here, piece[None], 0.0).reshape(tile_rows, half)

    kept, sent = kept_and_sent(part_of(own, low_group, own_offset))
    image = kept + swap(sent.astype(narrow), "col", 1).astype(jnp.float32)
    y1_one, y1_two = [scales[0] * image for image in sum_over("col", z_bits, *halves(image))]
    own, _ = lax.optimization_barrier((own, image))
    other = swap(own, "col", 1)
    part_own, part_other = backward(
        jnp.concatenate([y1_one.astype(narrow), y1_two.astype(narrow)]), own, other
    )
    y2_own, y2_other = sum_over(
        "row",
        row_bits,
        scales[1] * part_own - carries[1] * placed(own_start),
        scales[1] * part_other - carries[1] * placed(other_start),
    )
    image_one, image_two = sum_over(
        "col",
        z_bits,
        *halves(
            part_of(own, y2_own.astype(narrow), own_offset)
            + part_of(other, y2_other.astype(narrow), other_offset)
        ),
    )
    low_one = (scales[2] * image_one - carries[2] * y1_one).astype(narrow)
    low_two = (scales[2] * image_two - carries[2] * y1_two).astype(narrow)
    part_own, part_other = backward(jnp.concatenate([low_one, low_two]), own, other)
    image_own, image_other = sum_over("row", row_bits, part_own, part_other)
    y4_own = scales[3] * image_own - carries[3] * y2_own
    y4_other = scales[3] * image_other - carries[3] * y2_other

    mine = jnp.concatenate([y4_own, y4_other])
    theirs = swap(jnp.concatenate([y4_other, y4_own]).astype(narrow), "col", 1).astype(jnp.float32)
    corner = exact_dot(mine, mine, ((0,), (0,)))
    cross = exact_dot(theirs, jnp.where(mine_first, mine, theirs), ((0,), (0,)))
    rows = lax.broadcasted_iota(jnp.int32, (half, half), 0)
    lanes = lax.broadcasted_iota(jnp.int32, (half, half), 1)
    packed = jnp.where(mine_first | (rows >= lanes), cross, corner)
    diagonal = jnp.sum(jnp.where(rows == lanes, corner, 0.0), axis=0, keepdims=True)
    total = jnp.concatenate([packed, jnp.pad(diagonal, ((0, 7), (0, 0)))])
    far_to_near = [*range(2, z_count), 1]
    total = sum(lax.optimization_barrier([swap(total, "col", 2 * k) for k in far_to_near]), total)
    partner = swap(total, "col", 1)
    orbital_count = piece_rows * row_count * col_count
    here = row_rank * piece_rows
    mine = lax.dynamic_slice_in_dim(mine, here, piece_rows, 0)
    theirs = lax.dynamic_slice_in_dim(theirs, here, piece_rows, 0)
    return orthonormal(total, partner, mine, theirs, mine_first, math.sqrt(orbital_count))


def solution(mesh):
    return jax.shard_map(
        on_device,
        mesh=mesh,
        in_specs=(P("row", "col", None, None), P("row", "col"), P(("col", "row"), None)),
        out_specs=P(("col", "row"), None),
        check_vma=False,
    )
```

```python
import math

import jax
import jax.numpy as jnp
from jax import lax
from jax.experimental import pallas as pl
from jax.experimental.pallas import tpu as pltpu
from jax.sharding import PartitionSpec as P

DEGREE = 4


LOWER = -2.0
CUTOFF = 0.0
UPPER = 2.0


def filter_coefs(degree):
    half_width = (UPPER - CUTOFF) / 2.0
    center = (UPPER + CUTOFF) / 2.0
    sigma_now = half_width / (LOWER - center)
    tau_value = 2.0 / sigma_now
    scales = [sigma_now / half_width]
    carries = [0.0]
    for number in range(1, degree):
        sigma_next = 1.0 / (tau_value - sigma_now)
        scales.append(2.0 * sigma_next / half_width)
        carries.append(sigma_now * sigma_next)
        sigma_now = sigma_next
    return (center, scales, carries)


def swap(value, axis, distance):
    count = lax.axis_size(axis)
    return lax.ppermute(value, axis, [(i, i ^ distance) for i in range(count)])


def bits_below(count):
    return [1 << n for n in range(count.bit_length() - 1)]


def partners(count):
    return [1, *range(count - 1, 1, -1)]


def in_order(values, rank):
    stacked = jnp.stack(list(values.values()))

    def value_of(index):
        place = rank ^ index
        for number, distance in enumerate(values):
            if number != distance:
                place = jnp.where((rank ^ index) == distance, number, place)
        return lax.dynamic_index_in_dim(stacked, place, 0, False)

    return jnp.concatenate([value_of(index) for index in range(len(values))])


def densify(blocks, col_index, tile_blocks):
    group_rows, slots, width, _ = blocks.shape
    slots = min(slots, tile_blocks)
    step = group_rows

    def kernel(index_ref, blocks_ref, tile_ref):
        nothing = jnp.zeros((width, width), blocks.dtype)
        for inner in range(step):
            places = [index_ref[pl.program_id(0) * step + inner, slot] for slot in range(slots)]
            places = [jnp.where(place >= 0, lax.rem(place, tile_blocks), -1) for place in places]
            for column in range(tile_blocks):
                value = nothing
                for slot in range(slots):
                    value = jnp.where(places[slot] == column, blocks_ref[inner, slot], value)
                tile_ref[inner * width : (inner + 1) * width, column * width : (column + 1) * width] = value

    return pl.pallas_call(
        kernel,
        grid_spec=pltpu.PrefetchScalarGridSpec(
            num_scalar_prefetch=1,
            grid=(group_rows // step,),
            in_specs=[pl.BlockSpec((step, slots, width, width), lambda i, index: (i, 0, 0, 0))],
            out_specs=pl.BlockSpec((step * width, tile_blocks * width), lambda i, index: (i, 0)),
        ),
        out_shape=jax.ShapeDtypeStruct((group_rows * width, tile_blocks * width), blocks.dtype),
        compiler_params=pltpu.CompilerParams(vmem_limit_bytes=24 << 20),
    )(col_index, blocks)


def exact_dot(a, b, dims):
    return lax.dot_general(
        a, b, (dims, ((), ())), precision=lax.Precision.HIGHEST, preferred_element_type=jnp.float32
    )


def tree_sum(terms):
    while len(terms) > 1:
        terms = [sum(terms[n + 1 : n + 2], terms[n]) for n in range(0, len(terms), 2)]
    return terms[0]


def factor(matrix, tall):
    size = matrix.shape[1]
    groups = [matrix[first : first + tall] for first in range(0, size, tall)]
    sub = lax.broadcasted_iota(jnp.int32, (tall, size), 0)
    lane = lax.broadcasted_iota(jnp.int32, (tall, size), 1)
    for number, head in enumerate(groups):
        first = tall * number
        block = (lane >= first) & (lane < first + tall)
        columns = [jnp.broadcast_to(head[:, first + q : first + q + 1], head.shape) for q in range(tall)]
        x = jnp.where(block, jnp.where(lane - first == sub, 1.0, 0.0), head)
        z = x
        pivots = jnp.ones_like(x)
        inverses = jnp.ones_like(x)
        for p in range(tall):
            pivot = columns[p][p : p + 1, :]
            inverse = 1.0 / pivot
            masked = jnp.where(sub == p, 0.0, columns[p])
            others = masked * inverse
            below = jnp.where(sub > p, others, 0.0)
            for q in range(p + 1, tall):
                if q == p + 1:
                    columns[q] = columns[q] - (masked * columns[q][p : p + 1, :]) * inverse
                else:
                    columns[q] = columns[q] - others * columns[q][p : p + 1, :]
            x = x - below * x[p : p + 1, :]
            z = z - others * z[p : p + 1, :]
            pivots = jnp.where(sub == p, pivot, pivots)
            inverses = jnp.where(sub == p, inverse, inverses)
        z = z * inverses
        if number + 1 < len(groups):
            following = groups[number + 1]
            terms = [following[:, first + p : first + p + 1] * z[p : p + 1, :] for p in range(tall)]
            groups[number + 1] = jnp.where(block, 0.0, following) - tree_sum(terms)
        if number + 2 < len(groups):
            rest = jnp.concatenate(groups[number + 2 :])
            lanes = lax.broadcasted_iota(jnp.int32, rest.shape, 1)
            gone = (lanes >= first) & (lanes < first + tall)
            placed = [jnp.zeros((first, size), jnp.float32)] if first else []
            placed = jnp.concatenate([*placed, z, jnp.zeros((size - first - tall, size), jnp.float32)])
            rest = jnp.where(gone, 0.0, rest) - exact_dot(rest, placed, ((1,), (0,)))
            groups[number + 2 :] = [rest[n : n + tall] for n in range(0, rest.shape[0], tall)]
        groups[number] = x * lax.rsqrt(pivots)
    return jnp.concatenate(groups)


def orthonormal(total, partner, mine, theirs, mine_first, scale):
    size = total.shape[1]
    tall = 16

    def kernel(first_ref, total_ref, partner_ref, mine_ref, theirs_ref, out_ref):
        rows = lax.broadcasted_iota(jnp.int32, (size, size), 0)
        lanes = lax.broadcasted_iota(jnp.int32, (size, size), 1)
        is_first = first_ref[0] != 0
        cross = jnp.where(is_first, total_ref[:size, :], partner_ref[:size, :])
        both = jnp.where(is_first, partner_ref[:size, :], total_ref[:size, :])
        diagonal = jnp.where(is_first, partner_ref[size : size + 1, :], total_ref[size : size + 1, :])
        mirrored = both.T
        first = factor(jnp.where(rows >= lanes, both, mirrored), tall)
        first = jnp.where(rows >= lanes, first, 0.0)
        below = exact_dot(cross, first, ((1,), (1,)))
        second = jnp.where(lanes > rows, both, mirrored)
        second = jnp.where(lanes == rows, diagonal, second)
        last = factor(second - exact_dot(below, below, ((1,), (1,))), tall)
        last = jnp.where(rows >= lanes, last, 0.0)
        left = jnp.where(is_first, mine_ref[...], theirs_ref[...])
        left = exact_dot(left, first, ((1,), (1,)))
        out_ref[:, :size] = scale * left
        right = jnp.where(is_first, theirs_ref[...], mine_ref[...]) - exact_dot(left, below, ((1,), (1,)))
        out_ref[:, size:] = scale * exact_dot(right, last, ((1,), (1,)))

    vmem = pl.BlockSpec(memory_space=pltpu.VMEM)
    return pl.pallas_call(
        kernel,
        in_specs=[pl.BlockSpec(memory_space=pltpu.SMEM), vmem, vmem, vmem, vmem],
        out_specs=vmem,
        out_shape=jax.ShapeDtypeStruct((mine.shape[0], 2 * size), jnp.float32),
        compiler_params=pltpu.CompilerParams(vmem_limit_bytes=8 << 20),
    )(mine_first.astype(jnp.int32).reshape(1), total, partner, mine, theirs)


def on_device(blocks, col_index, vectors):
    center, scales, carries = filter_coefs(DEGREE)
    row_count = lax.axis_size("row")
    col_count = lax.axis_size("col")
    row_rank = lax.axis_index("row")
    col_rank = lax.axis_index("col")
    core = col_rank % 2
    group_rows, _, width, _ = blocks.shape
    piece_rows, states = vectors.shape
    half = states // 2
    tile_blocks = piece_rows // width * row_count
    tile_rows = tile_blocks * width
    row_bits = bits_below(row_count)
    z_count = col_count // 2
    z_bits = [2 * bit for bit in bits_below(z_count)]
    narrow = jnp.bfloat16

    mine_first = core == 0

    def kept_and_sent(value):
        left, right = value[:, :half], value[:, half:]
        return jnp.where(mine_first, left, right), jnp.where(mine_first, right, left)

    low_start = lax.optimization_barrier(vectors.astype(narrow))
    arrived = {0: low_start, **{k: swap(low_start, "row", k) for k in partners(row_count)}}
    low_group = in_order(arrived, row_rank)
    own_start, sent = kept_and_sent(vectors)
    other_start = swap(sent, "col", 1)

    own = densify(blocks, col_index, tile_blocks)

    first_row = row_rank * group_rows
    own_offset = first_row - col_rank * tile_blocks
    other_offset = first_row - (col_rank ^ 1) * tile_blocks

    segments = group_rows // tile_blocks

    def spread(low, offset):
        value = low.astype(jnp.float32)
        return jnp.concatenate(
            [jnp.where(offset == -k * tile_blocks, value, 0.0) for k in range(segments)]
        )

    def picked(low, offset):
        value = low.astype(jnp.float32).reshape(segments, tile_rows, low.shape[1])
        parts = [jnp.where(offset == -k * tile_blocks, value[k], 0.0) for k in range(segments)]
        return sum(parts[1:], parts[0])

    def halves(value):
        middle = value.shape[0] // 2
        return value[:middle], value[middle:]

    def part_of(tile, low, offset):
        product = jnp.dot(tile, low, preferred_element_type=jnp.float32)
        return product - center * spread(low, offset)

    def backward(low, own, other):
        def part(tile, offset):
            product = lax.dot_general(tile, low, (((0,), (0,)), ((), ())), preferred_element_type=jnp.float32)
            return product - center * picked(low, offset)

        return part(own, own_offset), part(other, other_offset)

    def sum_over(axis, bits, one, two):
        for bit_one, bit_two in zip(bits, reversed(bits)):
            from_one = swap(one.astype(narrow), axis, bit_one)
            from_two = swap(two.astype(narrow), axis, bit_two)
            if axis == "col" or bit_one != bits[-1]:
                from_one, from_two = lax.optimization_barrier((from_one, from_two))
            one, two = one + from_one.astype(jnp.float32), two + from_two.astype(jnp.float32)
        return one, two

    def placed(piece):
        here = jnp.arange(row_count)[:, None, None] == row_rank
        return jnp.where(here, piece[None], 0.0).reshape(tile_rows, half)

    kept, sent = kept_and_sent(part_of(own, low_group, own_offset))
    image = kept + swap(sent.astype(narrow), "col", 1).astype(jnp.float32)
    y1_one, y1_two = [scales[0] * image for image in sum_over("col", z_bits, *halves(image))]
    own, _ = lax.optimization_barrier((own, image))
    other = swap(own, "col", 1)
    part_own, part_other = backward(
        jnp.concatenate([y1_one.astype(narrow), y1_two.astype(narrow)]), own, other
    )
    y2_own, y2_other = sum_over(
        "row",
        row_bits,
        scales[1] * part_own - carries[1] * placed(own_start),
        scales[1] * part_other - carries[1] * placed(other_start),
    )
    image_one, image_two = sum_over(
        "col",
        z_bits,
        *halves(
            part_of(own, y2_own.astype(narrow), own_offset)
            + part_of(other, y2_other.astype(narrow), other_offset)
        ),
    )
    low_one = (scales[2] * image_one - carries[2] * y1_one).astype(narrow)
    low_two = (scales[2] * image_two - carries[2] * y1_two).astype(narrow)
    part_own, part_other = backward(jnp.concatenate([low_one, low_two]), own, other)
    image_own, image_other = sum_over("row", row_bits, part_own, part_other)
    y4_own = scales[3] * image_own - carries[3] * y2_own
    y4_other = scales[3] * image_other - carries[3] * y2_other

    mine = jnp.concatenate([y4_own, y4_other])
    theirs = swap(jnp.concatenate([y4_other, y4_own]).astype(narrow), "col", 1).astype(jnp.float32)
    corner = exact_dot(mine, mine, ((0,), (0,)))
    cross = exact_dot(theirs, jnp.where(mine_first, mine, theirs), ((0,), (0,)))
    rows = lax.broadcasted_iota(jnp.int32, (half, half), 0)
    lanes = lax.broadcasted_iota(jnp.int32, (half, half), 1)
    packed = jnp.where(mine_first | (rows >= lanes), cross, corner)
    diagonal = jnp.sum(jnp.where(rows == lanes, corner, 0.0), axis=0, keepdims=True)
    total = jnp.concatenate([packed, jnp.pad(diagonal, ((0, 7), (0, 0)))])
    far_to_near = range(z_count - 1, 0, -1)
    total = sum(lax.optimization_barrier([swap(total, "col", 2 * k) for k in far_to_near]), total)
    partner = swap(total, "col", 1)
    orbital_count = piece_rows * row_count * col_count
    here = row_rank * piece_rows
    mine = lax.dynamic_slice_in_dim(mine, here, piece_rows, 0)
    theirs = lax.dynamic_slice_in_dim(theirs, here, piece_rows, 0)
    return orthonormal(total, partner, mine, theirs, mine_first, math.sqrt(orbital_count))


def solution(mesh):
    return jax.shard_map(
        on_device,
        mesh=mesh,
        in_specs=(P("row", "col", None, None), P("row", "col"), P(("col", "row"), None)),
        out_specs=P(("col", "row"), None),
        check_vma=False,
    )
```

```python
import math

import jax
import jax.numpy as jnp
from jax import lax
from jax.experimental import pallas as pl
from jax.experimental.pallas import tpu as pltpu
from jax.sharding import PartitionSpec as P

DEGREE = 4


LOWER = -2.0
CUTOFF = 0.0
UPPER = 2.0


def filter_coefs(degree):
    half_width = (UPPER - CUTOFF) / 2.0
    center = (UPPER + CUTOFF) / 2.0
    sigma_now = half_width / (LOWER - center)
    tau_value = 2.0 / sigma_now
    scales = [sigma_now / half_width]
    carries = [0.0]
    for number in range(1, degree):
        sigma_next = 1.0 / (tau_value - sigma_now)
        scales.append(2.0 * sigma_next / half_width)
        carries.append(sigma_now * sigma_next)
        sigma_now = sigma_next
    return (center, scales, carries)


def swap(value, axis, distance):
    count = lax.axis_size(axis)
    return lax.ppermute(value, axis, [(i, i ^ distance) for i in range(count)])


def bits_below(count):
    return [1 << n for n in range(count.bit_length() - 1)]


def partners(count):
    return [1, *range(count - 1, 1, -1)]


def in_order(values, rank):
    stacked = jnp.stack(list(values.values()))

    def value_of(index):
        place = rank ^ index
        for number, distance in enumerate(values):
            if number != distance:
                place = jnp.where((rank ^ index) == distance, number, place)
        return lax.dynamic_index_in_dim(stacked, place, 0, False)

    return jnp.concatenate([value_of(index) for index in range(len(values))])


def densify(blocks, col_index, tile_blocks):
    group_rows, slots, width, _ = blocks.shape
    slots = min(slots, tile_blocks)
    step = group_rows

    def kernel(index_ref, blocks_ref, tile_ref):
        nothing = jnp.zeros((width, width), blocks.dtype)
        for inner in range(step):
            places = [index_ref[inner, slot] for slot in range(slots)]
            places = [jnp.where(place >= 0, lax.rem(place, tile_blocks), -1) for place in places]
            for column in range(tile_blocks):
                value = nothing
                for slot in range(slots):
                    value = jnp.where(places[slot] == column, blocks_ref[inner, slot], value)
                tile_ref[inner * width : (inner + 1) * width, column * width : (column + 1) * width] = value

    return pl.pallas_call(
        kernel,
        in_specs=[pl.BlockSpec(memory_space=pltpu.SMEM), pl.BlockSpec(memory_space=pltpu.VMEM)],
        out_specs=pl.BlockSpec(memory_space=pltpu.VMEM),
        out_shape=jax.ShapeDtypeStruct((group_rows * width, tile_blocks * width), blocks.dtype),
        compiler_params=pltpu.CompilerParams(vmem_limit_bytes=24 << 20),
    )(col_index, blocks)


def exact_dot(a, b, dims):
    return lax.dot_general(
        a, b, (dims, ((), ())), precision=lax.Precision.HIGHEST, preferred_element_type=jnp.float32
    )


def tree_sum(terms):
    while len(terms) > 1:
        terms = [sum(terms[n + 1 : n + 2], terms[n]) for n in range(0, len(terms), 2)]
    return terms[0]


def factor(matrix, tall):
    size = matrix.shape[1]
    groups = [matrix[first : first + tall] for first in range(0, size, tall)]
    sub = lax.broadcasted_iota(jnp.int32, (tall, size), 0)
    lane = lax.broadcasted_iota(jnp.int32, (tall, size), 1)
    for number, head in enumerate(groups):
        first = tall * number
        block = (lane >= first) & (lane < first + tall)
        columns = [jnp.broadcast_to(head[:, first + q : first + q + 1], head.shape) for q in range(tall)]
        x = jnp.where(block, jnp.where(lane - first == sub, 1.0, 0.0), head)
        z = x
        pivots = jnp.ones_like(x)
        inverses = jnp.ones_like(x)
        for p in range(tall):
            pivot = columns[p][p : p + 1, :]
            inverse = 1.0 / pivot
            masked = jnp.where(sub == p, 0.0, columns[p])
            others = masked * inverse
            below = jnp.where(sub > p, others, 0.0)
            for q in range(p + 1, tall):
                if q == p + 1:
                    columns[q] = columns[q] - (masked * columns[q][p : p + 1, :]) * inverse
                else:
                    columns[q] = columns[q] - others * columns[q][p : p + 1, :]
            x = x - below * x[p : p + 1, :]
            z = z - others * z[p : p + 1, :]
            pivots = jnp.where(sub == p, pivot, pivots)
            inverses = jnp.where(sub == p, inverse, inverses)
        z = z * inverses
        if number + 1 < len(groups):
            following = groups[number + 1]
            terms = [following[:, first + p : first + p + 1] * z[p : p + 1, :] for p in range(tall)]
            groups[number + 1] = jnp.where(block, 0.0, following) - tree_sum(terms)
        if number + 2 < len(groups):
            rest = jnp.concatenate(groups[number + 2 :])
            lanes = lax.broadcasted_iota(jnp.int32, rest.shape, 1)
            gone = (lanes >= first) & (lanes < first + tall)
            placed = [jnp.zeros((first, size), jnp.float32)] if first else []
            placed = jnp.concatenate([*placed, z, jnp.zeros((size - first - tall, size), jnp.float32)])
            rest = jnp.where(gone, 0.0, rest) - exact_dot(rest, placed, ((1,), (0,)))
            groups[number + 2 :] = [rest[n : n + tall] for n in range(0, rest.shape[0], tall)]
        groups[number] = x * lax.rsqrt(pivots)
    return jnp.concatenate(groups)


def orthonormal(total, partner, mine, theirs, mine_first, scale):
    size = total.shape[1]
    tall = 16

    def kernel(first_ref, total_ref, partner_ref, mine_ref, theirs_ref, out_ref):
        rows = lax.broadcasted_iota(jnp.int32, (size, size), 0)
        lanes = lax.broadcasted_iota(jnp.int32, (size, size), 1)
        is_first = first_ref[0] != 0
        cross = jnp.where(is_first, total_ref[:size, :], partner_ref[:size, :])
        both = jnp.where(is_first, partner_ref[:size, :], total_ref[:size, :])
        diagonal = jnp.where(is_first, partner_ref[size : size + 1, :], total_ref[size : size + 1, :])
        mirrored = both.T
        first = factor(jnp.where(rows >= lanes, both, mirrored), tall)
        first = jnp.where(rows >= lanes, first, 0.0)
        below = exact_dot(cross, first, ((1,), (1,)))
        second = jnp.where(lanes > rows, both, mirrored)
        second = jnp.where(lanes == rows, diagonal, second)
        last = factor(second - exact_dot(below, below, ((1,), (1,))), tall)
        last = jnp.where(rows >= lanes, last, 0.0)
        left = jnp.where(is_first, mine_ref[...], theirs_ref[...])
        left = exact_dot(left, first, ((1,), (1,)))
        out_ref[:, :size] = scale * left
        right = jnp.where(is_first, theirs_ref[...], mine_ref[...]) - exact_dot(left, below, ((1,), (1,)))
        out_ref[:, size:] = scale * exact_dot(right, last, ((1,), (1,)))

    vmem = pl.BlockSpec(memory_space=pltpu.VMEM)
    return pl.pallas_call(
        kernel,
        in_specs=[pl.BlockSpec(memory_space=pltpu.SMEM), vmem, vmem, vmem, vmem],
        out_specs=vmem,
        out_shape=jax.ShapeDtypeStruct((mine.shape[0], 2 * size), jnp.float32),
        compiler_params=pltpu.CompilerParams(vmem_limit_bytes=8 << 20),
    )(mine_first.astype(jnp.int32).reshape(1), total, partner, mine, theirs)


def on_device(blocks, col_index, vectors):
    center, scales, carries = filter_coefs(DEGREE)
    row_count = lax.axis_size("row")
    col_count = lax.axis_size("col")
    row_rank = lax.axis_index("row")
    col_rank = lax.axis_index("col")
    core = col_rank % 2
    group_rows, _, width, _ = blocks.shape
    piece_rows, states = vectors.shape
    half = states // 2
    tile_blocks = piece_rows // width * row_count
    tile_rows = tile_blocks * width
    row_bits = bits_below(row_count)
    z_count = col_count // 2
    z_bits = [2 * bit for bit in bits_below(z_count)]
    narrow = jnp.bfloat16

    mine_first = core == 0

    def kept_and_sent(value):
        left, right = value[:, :half], value[:, half:]
        return jnp.where(mine_first, left, right), jnp.where(mine_first, right, left)

    low_start = lax.optimization_barrier(vectors.astype(narrow))
    arrived = {0: low_start, **{k: swap(low_start, "row", k) for k in partners(row_count)}}
    low_group = in_order(arrived, row_rank)
    own_start, sent = kept_and_sent(vectors)
    other_start = swap(sent, "col", 1)

    own = densify(blocks, col_index, tile_blocks)

    first_row = row_rank * group_rows
    own_offset = first_row - col_rank * tile_blocks
    other_offset = first_row - (col_rank ^ 1) * tile_blocks

    segments = group_rows // tile_blocks

    def spread(low, offset):
        value = low.astype(jnp.float32)
        return jnp.concatenate(
            [jnp.where(offset == -k * tile_blocks, value, 0.0) for k in range(segments)]
        )

    def picked(low, offset):
        value = low.astype(jnp.float32).reshape(segments, tile_rows, low.shape[1])
        parts = [jnp.where(offset == -k * tile_blocks, value[k], 0.0) for k in range(segments)]
        return sum(parts[1:], parts[0])

    def halves(value):
        middle = value.shape[0] // 2
        return value[:middle], value[middle:]

    def part_of(tile, low, offset):
        product = jnp.dot(tile, low, preferred_element_type=jnp.float32)
        return product - center * spread(low, offset)

    def backward(low, own, other):
        def part(tile, offset):
            product = lax.dot_general(tile, low, (((0,), (0,)), ((), ())), preferred_element_type=jnp.float32)
            return product - center * picked(low, offset)

        return part(own, own_offset), part(other, other_offset)

    def sum_over(axis, bits, one, two):
        for bit_one, bit_two in zip(bits, reversed(bits)):
            from_one = swap(one.astype(narrow), axis, bit_one)
            from_two = swap(two.astype(narrow), axis, bit_two)
            if axis == "col" or bit_one != bits[-1]:
                from_one, from_two = lax.optimization_barrier((from_one, from_two))
            one, two = one + from_one.astype(jnp.float32), two + from_two.astype(jnp.float32)
        return one, two

    def placed(piece):
        here = jnp.arange(row_count)[:, None, None] == row_rank
        return jnp.where(here, piece[None], 0.0).reshape(tile_rows, half)

    kept, sent = kept_and_sent(part_of(own, low_group, own_offset))
    image = kept + swap(sent.astype(narrow), "col", 1).astype(jnp.float32)
    y1_one, y1_two = [scales[0] * image for image in sum_over("col", z_bits, *halves(image))]
    own, _ = lax.optimization_barrier((own, image))
    other = swap(own, "col", 1)
    part_own, part_other = backward(
        jnp.concatenate([y1_one.astype(narrow), y1_two.astype(narrow)]), own, other
    )
    y2_own, y2_other = sum_over(
        "row",
        row_bits,
        scales[1] * part_own - carries[1] * placed(own_start),
        scales[1] * part_other - carries[1] * placed(other_start),
    )
    image_one, image_two = sum_over(
        "col",
        z_bits,
        *halves(
            part_of(own, y2_own.astype(narrow), own_offset)
            + part_of(other, y2_other.astype(narrow), other_offset)
        ),
    )
    low_one = (scales[2] * image_one - carries[2] * y1_one).astype(narrow)
    low_two = (scales[2] * image_two - carries[2] * y1_two).astype(narrow)
    part_own, part_other = backward(jnp.concatenate([low_one, low_two]), own, other)
    image_own, image_other = sum_over("row", row_bits, part_own, part_other)
    y4_own = scales[3] * image_own - carries[3] * y2_own
    y4_other = scales[3] * image_other - carries[3] * y2_other

    mine = jnp.concatenate([y4_own, y4_other])
    theirs = swap(jnp.concatenate([y4_other, y4_own]).astype(narrow), "col", 1).astype(jnp.float32)
    corner = exact_dot(mine, mine, ((0,), (0,)))
    cross = exact_dot(theirs, jnp.where(mine_first, mine, theirs), ((0,), (0,)))
    rows = lax.broadcasted_iota(jnp.int32, (half, half), 0)
    lanes = lax.broadcasted_iota(jnp.int32, (half, half), 1)
    packed = jnp.where(mine_first | (rows >= lanes), cross, corner)
    diagonal = jnp.sum(jnp.where(rows == lanes, corner, 0.0), axis=0, keepdims=True)
    total = jnp.concatenate([packed, jnp.pad(diagonal, ((0, 7), (0, 0)))])
    far_to_near = range(z_count - 1, 0, -1)
    total = sum(lax.optimization_barrier([swap(total, "col", 2 * k) for k in far_to_near]), total)
    partner = swap(total, "col", 1)
    orbital_count = piece_rows * row_count * col_count
    here = row_rank * piece_rows
    mine = lax.dynamic_slice_in_dim(mine, here, piece_rows, 0)
    theirs = lax.dynamic_slice_in_dim(theirs, here, piece_rows, 0)
    return orthonormal(total, partner, mine, theirs, mine_first, math.sqrt(orbital_count))


def solution(mesh):
    return jax.shard_map(
        on_device,
        mesh=mesh,
        in_specs=(P("row", "col", None, None), P("row", "col"), P(("col", "row"), None)),
        out_specs=P(("col", "row"), None),
        check_vma=False,
    )
```

```python
import math

import jax
import jax.numpy as jnp
from jax import lax
from jax.experimental import pallas as pl
from jax.experimental.pallas import tpu as pltpu
from jax.sharding import PartitionSpec as P

DEGREE = 4


LOWER = -2.0
CUTOFF = 0.0
UPPER = 2.0


def filter_coefs(degree):
    half_width = (UPPER - CUTOFF) / 2.0
    center = (UPPER + CUTOFF) / 2.0
    sigma_now = half_width / (LOWER - center)
    tau_value = 2.0 / sigma_now
    scales = [sigma_now / half_width]
    carries = [0.0]
    for number in range(1, degree):
        sigma_next = 1.0 / (tau_value - sigma_now)
        scales.append(2.0 * sigma_next / half_width)
        carries.append(sigma_now * sigma_next)
        sigma_now = sigma_next
    return (center, scales, carries)


def swap(value, axis, distance):
    count = lax.axis_size(axis)
    return lax.ppermute(value, axis, [(i, i ^ distance) for i in range(count)])


def bits_below(count):
    return [1 << n for n in range(count.bit_length() - 1)]


def partners(count):
    return [1, *range(count - 1, 1, -1)]


def in_order(values, rank):
    stacked = jnp.stack(list(values.values()))

    def value_of(index):
        place = rank ^ index
        for number, distance in enumerate(values):
            if number != distance:
                place = jnp.where((rank ^ index) == distance, number, place)
        return lax.dynamic_index_in_dim(stacked, place, 0, False)

    return jnp.concatenate([value_of(index) for index in range(len(values))])


def densify(blocks, col_index, tile_blocks):
    group_rows, slots, width, _ = blocks.shape
    slots = min(slots, tile_blocks)
    step = group_rows

    def kernel(index_ref, blocks_ref, tile_ref):
        nothing = jnp.zeros((width, width), blocks.dtype)
        for inner in range(step):
            places = [index_ref[inner, slot] for slot in range(slots)]
            places = [jnp.where(place >= 0, lax.rem(place, tile_blocks), -1) for place in places]
            for column in range(tile_blocks):
                value = nothing
                for slot in range(slots):
                    value = jnp.where(places[slot] == column, blocks_ref[inner, slot], value)
                tile_ref[inner * width : (inner + 1) * width, column * width : (column + 1) * width] = value

    return pl.pallas_call(
        kernel,
        in_specs=[pl.BlockSpec(memory_space=pltpu.SMEM), pl.BlockSpec(memory_space=pltpu.VMEM)],
        out_specs=pl.BlockSpec(memory_space=pltpu.VMEM),
        out_shape=jax.ShapeDtypeStruct((group_rows * width, tile_blocks * width), blocks.dtype),
        compiler_params=pltpu.CompilerParams(vmem_limit_bytes=24 << 20),
    )(col_index, blocks)


def exact_dot(a, b, dims):
    return lax.dot_general(
        a, b, (dims, ((), ())), precision=lax.Precision.HIGHEST, preferred_element_type=jnp.float32
    )


def tree_sum(terms):
    while len(terms) > 1:
        terms = [sum(terms[n + 1 : n + 2], terms[n]) for n in range(0, len(terms), 2)]
    return terms[0]


def factor(matrix, tall):
    size = matrix.shape[1]
    groups = [matrix[first : first + tall] for first in range(0, size, tall)]
    sub = lax.broadcasted_iota(jnp.int32, (tall, size), 0)
    lane = lax.broadcasted_iota(jnp.int32, (tall, size), 1)
    for number, head in enumerate(groups):
        first = tall * number
        block = (lane >= first) & (lane < first + tall)
        columns = [jnp.broadcast_to(head[:, first + q : first + q + 1], head.shape) for q in range(tall)]
        x = jnp.where(block, jnp.where(lane - first == sub, 1.0, 0.0), head)
        z = x
        pivots = jnp.ones_like(x)
        straight = jnp.zeros_like(x)
        crossed = jnp.zeros_like(x)
        for p in range(0, tall, 2):
            s = p + 1
            here, after = sub == p, sub == s
            a, b, c = columns[p][p : p + 1, :], columns[p][s : s + 1, :], columns[s][s : s + 1, :]
            inverse = 1.0 / (a * c - b * b)
            ratio = b / a
            from_p = jnp.where(here | after, 0.0, columns[p] * c - columns[s] * b)
            from_s = jnp.where(here | after, 0.0, columns[s] * a - columns[p] * b)
            by_p, by_s = from_p * inverse, from_s * inverse
            for q in range(p + 2, tall):
                row_p, row_s = columns[q][p : p + 1, :], columns[q][s : s + 1, :]
                if q < p + 4:
                    columns[q] = columns[q] - (from_p * row_p + from_s * row_s) * inverse
                else:
                    columns[q] = columns[q] - by_p * row_p - by_s * row_s
            x_p, x_s = x[p : p + 1, :], x[s : s + 1, :]
            below = sub > s
            x = x - jnp.where(below, by_p, jnp.where(after, ratio, 0.0)) * x_p - jnp.where(below, by_s, 0.0) * x_s
            z = z - by_p * z[p : p + 1, :] - by_s * z[s : s + 1, :]
            pivots = jnp.where(here, a, jnp.where(after, c - b * ratio, pivots))
            straight = jnp.where(here, c * inverse, jnp.where(after, a * inverse, straight))
            crossed = jnp.where(here | after, b * inverse, crossed)
        turned = jnp.where(sub % 2 == 0, pltpu.roll(z, tall - 1, 0), pltpu.roll(z, 1, 0))
        z = z * straight - turned * crossed
        if number + 1 < len(groups):
            following = groups[number + 1]
            terms = [following[:, first + p : first + p + 1] * z[p : p + 1, :] for p in range(tall)]
            groups[number + 1] = jnp.where(block, 0.0, following) - tree_sum(terms)
        if number + 2 < len(groups):
            rest = jnp.concatenate(groups[number + 2 :])
            lanes = lax.broadcasted_iota(jnp.int32, rest.shape, 1)
            gone = (lanes >= first) & (lanes < first + tall)
            placed = [jnp.zeros((first, size), jnp.float32)] if first else []
            placed = jnp.concatenate([*placed, z, jnp.zeros((size - first - tall, size), jnp.float32)])
            rest = jnp.where(gone, 0.0, rest) - exact_dot(rest, placed, ((1,), (0,)))
            groups[number + 2 :] = [rest[n : n + tall] for n in range(0, rest.shape[0], tall)]
        groups[number] = x * lax.rsqrt(pivots)
    return jnp.concatenate(groups)


def orthonormal(total, partner, mine, theirs, mine_first, scale):
    size = total.shape[1]
    tall = 16

    def kernel(first_ref, total_ref, partner_ref, mine_ref, theirs_ref, out_ref):
        rows = lax.broadcasted_iota(jnp.int32, (size, size), 0)
        lanes = lax.broadcasted_iota(jnp.int32, (size, size), 1)
        is_first = first_ref[0] != 0
        cross = jnp.where(is_first, total_ref[:size, :], partner_ref[:size, :])
        both = jnp.where(is_first, partner_ref[:size, :], total_ref[:size, :])
        diagonal = jnp.where(is_first, partner_ref[size : size + 1, :], total_ref[size : size + 1, :])
        mirrored = both.T
        first = factor(jnp.where(rows >= lanes, both, mirrored), tall)
        first = jnp.where(rows >= lanes, first, 0.0)
        below = exact_dot(cross, first, ((1,), (1,)))
        second = jnp.where(lanes > rows, both, mirrored)
        second = jnp.where(lanes == rows, diagonal, second)
        last = factor(second - exact_dot(below, below, ((1,), (1,))), tall)
        last = jnp.where(rows >= lanes, last, 0.0)
        left = jnp.where(is_first, mine_ref[...], theirs_ref[...])
        left = exact_dot(left, first, ((1,), (1,)))
        out_ref[:, :size] = scale * left
        right = jnp.where(is_first, theirs_ref[...], mine_ref[...]) - exact_dot(left, below, ((1,), (1,)))
        out_ref[:, size:] = scale * exact_dot(right, last, ((1,), (1,)))

    vmem = pl.BlockSpec(memory_space=pltpu.VMEM)
    return pl.pallas_call(
        kernel,
        in_specs=[pl.BlockSpec(memory_space=pltpu.SMEM), vmem, vmem, vmem, vmem],
        out_specs=vmem,
        out_shape=jax.ShapeDtypeStruct((mine.shape[0], 2 * size), jnp.float32),
        compiler_params=pltpu.CompilerParams(vmem_limit_bytes=8 << 20),
    )(mine_first.astype(jnp.int32).reshape(1), total, partner, mine, theirs)


def on_device(blocks, col_index, vectors):
    center, scales, carries = filter_coefs(DEGREE)
    row_count = lax.axis_size("row")
    col_count = lax.axis_size("col")
    row_rank = lax.axis_index("row")
    col_rank = lax.axis_index("col")
    core = col_rank % 2
    group_rows, _, width, _ = blocks.shape
    piece_rows, states = vectors.shape
    half = states // 2
    tile_blocks = piece_rows // width * row_count
    tile_rows = tile_blocks * width
    row_bits = bits_below(row_count)
    z_count = col_count // 2
    z_bits = [2 * bit for bit in bits_below(z_count)]
    narrow = jnp.bfloat16

    mine_first = core == 0

    def kept_and_sent(value):
        left, right = value[:, :half], value[:, half:]
        return jnp.where(mine_first, left, right), jnp.where(mine_first, right, left)

    low_start = lax.optimization_barrier(vectors.astype(narrow))
    arrived = {0: low_start, **{k: swap(low_start, "row", k) for k in partners(row_count)}}
    low_group = in_order(arrived, row_rank)
    own_start, sent = kept_and_sent(vectors)
    other_start = swap(sent, "col", 1)

    own = densify(blocks, col_index, tile_blocks)

    first_row = row_rank * group_rows
    own_offset = first_row - col_rank * tile_blocks
    other_offset = first_row - (col_rank ^ 1) * tile_blocks

    segments = group_rows // tile_blocks

    def spread(low, offset):
        value = low.astype(jnp.float32)
        return jnp.concatenate(
            [jnp.where(offset == -k * tile_blocks, value, 0.0) for k in range(segments)]
        )

    def picked(low, offset):
        value = low.astype(jnp.float32).reshape(segments, tile_rows, low.shape[1])
        parts = [jnp.where(offset == -k * tile_blocks, value[k], 0.0) for k in range(segments)]
        return sum(parts[1:], parts[0])

    def halves(value):
        middle = value.shape[0] // 2
        return value[:middle], value[middle:]

    def part_of(tile, low, offset):
        product = jnp.dot(tile, low, preferred_element_type=jnp.float32)
        return product - center * spread(low, offset)

    def backward(low, own, other):
        def part(tile, offset):
            product = lax.dot_general(tile, low, (((0,), (0,)), ((), ())), preferred_element_type=jnp.float32)
            return product - center * picked(low, offset)

        return part(own, own_offset), part(other, other_offset)

    def sum_over(axis, bits, one, two):
        for bit_one, bit_two in zip(bits, reversed(bits)):
            from_one = swap(one.astype(narrow), axis, bit_one)
            from_two = swap(two.astype(narrow), axis, bit_two)
            if axis == "col" or bit_one != bits[-1]:
                from_one, from_two = lax.optimization_barrier((from_one, from_two))
            one, two = one + from_one.astype(jnp.float32), two + from_two.astype(jnp.float32)
        return one, two

    def placed(piece):
        here = jnp.arange(row_count)[:, None, None] == row_rank
        return jnp.where(here, piece[None], 0.0).reshape(tile_rows, half)

    kept, sent = kept_and_sent(part_of(own, low_group, own_offset))
    image = kept + swap(sent.astype(narrow), "col", 1).astype(jnp.float32)
    y1_one, y1_two = [scales[0] * image for image in sum_over("col", z_bits, *halves(image))]
    own, _ = lax.optimization_barrier((own, image))
    other = swap(own, "col", 1)
    part_own, part_other = backward(
        jnp.concatenate([y1_one.astype(narrow), y1_two.astype(narrow)]), own, other
    )
    y2_own, y2_other = sum_over(
        "row",
        row_bits,
        scales[1] * part_own - carries[1] * placed(own_start),
        scales[1] * part_other - carries[1] * placed(other_start),
    )
    image_one, image_two = sum_over(
        "col",
        z_bits,
        *halves(
            part_of(own, y2_own.astype(narrow), own_offset)
            + part_of(other, y2_other.astype(narrow), other_offset)
        ),
    )
    low_one = (scales[2] * image_one - carries[2] * y1_one).astype(narrow)
    low_two = (scales[2] * image_two - carries[2] * y1_two).astype(narrow)
    part_own, part_other = backward(jnp.concatenate([low_one, low_two]), own, other)
    image_own, image_other = sum_over("row", row_bits, part_own, part_other)
    y4_own = scales[3] * image_own - carries[3] * y2_own
    y4_other = scales[3] * image_other - carries[3] * y2_other

    mine = jnp.concatenate([y4_own, y4_other])
    theirs = swap(jnp.concatenate([y4_other, y4_own]).astype(narrow), "col", 1).astype(jnp.float32)
    corner = exact_dot(mine, mine, ((0,), (0,)))
    cross = exact_dot(theirs, jnp.where(mine_first, mine, theirs), ((0,), (0,)))
    rows = lax.broadcasted_iota(jnp.int32, (half, half), 0)
    lanes = lax.broadcasted_iota(jnp.int32, (half, half), 1)
    packed = jnp.where(mine_first | (rows >= lanes), cross, corner)
    diagonal = jnp.sum(jnp.where(rows == lanes, corner, 0.0), axis=0, keepdims=True)
    total = jnp.concatenate([packed, jnp.pad(diagonal, ((0, 7), (0, 0)))])
    far_to_near = range(z_count - 1, 0, -1)
    total = sum(lax.optimization_barrier([swap(total, "col", 2 * k) for k in far_to_near]), total)
    partner = swap(total, "col", 1)
    orbital_count = piece_rows * row_count * col_count
    here = row_rank * piece_rows
    mine = lax.dynamic_slice_in_dim(mine, here, piece_rows, 0)
    theirs = lax.dynamic_slice_in_dim(theirs, here, piece_rows, 0)
    return orthonormal(total, partner, mine, theirs, mine_first, math.sqrt(orbital_count))


def solution(mesh):
    return jax.shard_map(
        on_device,
        mesh=mesh,
        in_specs=(P("row", "col", None, None), P("row", "col"), P(("col", "row"), None)),
        out_specs=P(("col", "row"), None),
        check_vma=False,
    )
```
